512 devices in a mesh: row: 16 (over z_lo, core), col: 32 (over x, y, z_hi).
Axes of the slice: x: 4, y: 4, z: 16 (z_hi: 2, z_lo: 8; z = z_hi * 8 + z_lo), core: 2. Of those that a mesh axis runs over, the one named last changes fastest.
Arguments:
- greens: float32 [13824, 13824], P('row', 'col')
- accepted_sites: int32 [256], replicated, may hold values from 0 to 13823, as said below
- field_values: int32 [256], replicated, may hold values from -1 to 1, as said below
- left_a: float32 [96, 144, 144], P('row')
- left_b: float32 [96, 144, 144], P('row')
- right_a: float32 [96, 144, 144], P('col')
- right_b: float32 [96, 144, 144], P('col')
Outputs:
- wrapped: float32 [13824, 13824], P('row', 'col')
The draws below stay inside these ranges and needn't reach their ends.
Inputs may be any that keep to these rules, and one draw needn't show every extreme that they name: `accepted_sites`: site k (from 0) lies in [k * 54, (k + 1) * 54), so the sites rise. `field_values`: each value is -1 or 1.
All inputs are finite; a program needn't handle non-finite values.
Results may differ from the reference program's by a relative error of at most 0.000073.
Values sent between devices are 32-bit elements; how exact they have to be, the bound alone decides.
A program may use at most 64 MiB of HBM per device.

```python
import jax
import jax.numpy as jnp
from jax import lax

CS = 144
CLUSTERS = 96
K = 256
N = 13824


def draw_greens(key, part):
    key_random = jax.random.fold_in(key, 11)
    key_diagonal = jax.random.fold_in(key, 12)
    random_part = jnp.clip(jax.random.normal(key_random, (N, N), jnp.float32), -4.0, 4.0)
    diagonal = jax.random.uniform(key_diagonal, (N,), jnp.float32, 0.3, 0.7)
    first_index = lax.broadcasted_iota(jnp.int32, (N, N), 0)
    second_index = lax.broadcasted_iota(jnp.int32, (N, N), 1)
    return jnp.where(first_index == second_index, diagonal[:, None], 0.006 * random_part)


def draw_accepted_sites(key, part):
    stride = N // K
    offsets = jax.random.randint(jax.random.fold_in(key, 21), (K,), 0, stride)
    return jnp.arange(K, dtype=jnp.int32) * stride + offsets


def draw_field_values(key, part):
    return 2 * jax.random.randint(jax.random.fold_in(key, 22), (K,), 0, 2) - 1


def propagator_blocks(key, salt):
    key_random = jax.random.fold_in(key, salt)
    key_diagonal = jax.random.fold_in(key, salt + 100)
    random_part = jnp.clip(jax.random.normal(key_random, (CLUSTERS, CS, CS), jnp.float32), -4.0, 4.0)
    diagonal = jax.random.uniform(key_diagonal, (CLUSTERS, CS, 1), jnp.float32, 0.8, 1.2)
    first_index = lax.broadcasted_iota(jnp.int32, (CLUSTERS, CS, CS), 1)
    second_index = lax.broadcasted_iota(jnp.int32, (CLUSTERS, CS, CS), 2)
    return jnp.where(first_index == second_index, diagonal, 0.05 * random_part)


def draw_left_a(key, part):
    return propagator_blocks(key, 31)


def draw_left_b(key, part):
    return propagator_blocks(key, 32)


def draw_right_a(key, part):
    return propagator_blocks(key, 33)


def draw_right_b(key, part):
    return propagator_blocks(key, 34)


def setup_inputs(seed: int = 0) -> dict:
    arg_keys = jax.random.split(jax.random.key(seed), 8)
    greens = draw_greens(jax.random.fold_in(arg_keys[7], 71), 0)
    accepted_sites = draw_accepted_sites(jax.random.fold_in(arg_keys[7], 71), 0)
    field_values = draw_field_values(jax.random.fold_in(arg_keys[7], 71), 0)
    left_a = draw_left_a(jax.random.fold_in(arg_keys[7], 71), 0)
    left_b = draw_left_b(jax.random.fold_in(arg_keys[7], 71), 0)
    right_a = draw_right_a(jax.random.fold_in(arg_keys[7], 71), 0)
    right_b = draw_right_b(jax.random.fold_in(arg_keys[7], 71), 0)
    return dict(greens=greens, accepted_sites=accepted_sites, field_values=field_values, left_a=left_a, left_b=left_b, right_a=right_a, right_b=right_b)


highest = lax.Precision.HIGHEST
coupling = 0.45

def blocks_left(blocks, matrix):
    number = blocks.shape[0]
    cluster = blocks.shape[1]
    product = jnp.einsum('cab,cbm->cam', blocks, matrix.reshape(number, cluster, matrix.shape[1]), precision=highest)
    return product.reshape(matrix.shape)

def blocks_right(matrix, blocks):
    number = blocks.shape[0]
    cluster = blocks.shape[1]
    product = jnp.einsum('mcb,cba->mca', matrix.reshape(matrix.shape[0], number, cluster), blocks, precision=highest)
    return product.reshape(matrix.shape)

def wrap_left(matrix, first_blocks, second_blocks):
    margin = first_blocks.shape[1] // 2
    inner = blocks_left(first_blocks, matrix)
    rolled = jnp.roll(inner, -margin, axis=0)
    return jnp.roll(blocks_left(second_blocks, rolled), margin, axis=0)

def wrap_right(matrix, first_blocks, second_blocks):
    margin = first_blocks.shape[1] // 2
    inner = blocks_right(matrix, first_blocks)
    rolled = jnp.roll(inner, -margin, axis=1)
    return jnp.roll(blocks_right(rolled, second_blocks), margin, axis=1)

def reference(greens, accepted_sites, field_values, left_a, left_b, right_a, right_b):
    shifts = jnp.exp(-2.0 * coupling * field_values.astype(jnp.float32)) - 1.0
    g_cols = jnp.take(greens, accepted_sites, axis=1)
    g_rows = jnp.take(greens, accepted_sites, axis=0)
    g_pair = jnp.take(g_rows, accepted_sites, axis=1)
    identity = jnp.eye(K, dtype=jnp.float32)
    capacity = identity + (identity - g_pair) * shifts[None, :]
    inverse = jnp.linalg.solve(capacity, identity)
    scaled = shifts[:, None] * inverse
    picked = (accepted_sites[:, None] == jnp.arange(N, dtype=jnp.int32)[None, :]).astype(jnp.float32)
    complement = picked - g_rows
    factor = jnp.dot(scaled, complement, precision=highest)
    updated = greens - jnp.dot(g_cols, factor, precision=highest)
    return wrap_right(wrap_left(updated, left_a, left_b), right_a, right_b)
```

```python
import functools

import jax
import jax.numpy as jnp
from jax import lax
from jax.experimental import pallas as pl
from jax.experimental.pallas import tpu as pltpu
from jax.sharding import PartitionSpec as P

MESH = pl.DeviceIdType.MESH
f32 = jnp.float32
high = lax.Precision.HIGH
highest = lax.Precision.HIGHEST
coupling = 0.45
series_bound = 1e-7

CS = 144
HALF = 72
ROWS, COLS = 16, 32
HEIGHT, WIDTH = 864, 432
K = 256
KR, KC = 16, 8
WIDE = 512
TALL = 896
EDGE = (0, 128, 768, HEIGHT)


def nn(a, b, precision=high):
    return lax.dot_general(a, b, (((1,), (0,)), ((), ())), precision=precision, preferred_element_type=f32)


def nt(a, b, precision=high):
    return lax.dot_general(a, b, (((1,), (1,)), ((), ())), precision=precision, preferred_element_type=f32)


def iota(shape, dim):
    return lax.broadcasted_iota(jnp.int32, shape, dim)


def exchange_kernel(
    sites, field, g, la, lb, ra, rb,
    acc_out, halo_out, wd_out, norm_out, t_out, u_out, v_out, gp_out,
    q, y, t, acc, qtop, pbot, pb_in, lq_s, lq_in, rq_s, rq_in, redge, redge_t, wd, bloc, rown,
    xs, x_in, edge, ubuf, u, vbuf, gbuf, gp, norm,
    es, er, hs, hr, xsem, xr, cs, cr, vs, vr, us, ur, gs, gr, outs,
):
    r = lax.axis_index("row")
    c = lax.axis_index("col")
    zl, core = r // 2, lax.rem(r, 2)
    zh, xy = lax.rem(c, 2), c // 2
    yy, xx = lax.rem(xy, 4), xy // 4
    rup, rdn = lax.rem(r + 1, ROWS), lax.rem(r + ROWS - 1, ROWS)
    cup, cdn = lax.rem(c + 1, COLS), lax.rem(c + COLS - 1, COLS)
    twin = (r + 1 - 2 * core, c)
    far = (r, c + 1 - 2 * zh)
    ypeer = [(r, (xx * 4 + lax.rem(yy + d, 4)) * 2 + zh) for d in (1, 2, 3)]
    xpeer = [(r, (lax.rem(xx + d, 4) * 4 + yy) * 2 + zh) for d in (1, 2, 3)]
    peers = [(rup, c), (rdn, c), (lax.rem(r + 2, ROWS), c), (lax.rem(r + ROWS - 2, ROWS), c), (r, cup), (r, cdn)]
    peers += ypeer + xpeer
    barrier = pltpu.get_barrier_semaphore()
    for peer in peers:
        pl.semaphore_signal(barrier, inc=1, device_id=peer, device_id_type=MESH)

    def remote(src, dst, send, recv, to):
        return pltpu.make_async_remote_copy(src, dst, send, recv, device_id=to, device_id_type=MESH)

    lane = iota((KR, WIDTH), 1)
    sub = iota((KR, WIDTH), 0)
    rows = jnp.zeros((KR, WIDTH), f32)
    where_site = jnp.full((KR, WIDTH), -1, jnp.int32)
    for j in range(KR):
        site = sites[r * KR + j]
        line = g[pl.ds(jnp.clip(site - r * HEIGHT, 0, HEIGHT - 1), 1), :]
        rows = jnp.where(sub == j, line, rows)
        where_site = jnp.where(sub == j, site - c * WIDTH, where_site)
    x = jnp.where(lane == where_site, 1.0, 0.0) - rows
    hit_lane = iota((128, WIDTH), 1)
    hit_sub = iota((128, WIDTH), 0)
    hit_site = jnp.full((128, WIDTH), -1, jnp.int32)
    for j in range(KC):
        hit_site = jnp.where(hit_sub == 48 + j, sites[c * KC + j] - c * WIDTH, hit_site)
    hit = jnp.where(hit_lane == hit_site, 1.0, 0.0)
    piece = nt(rows, hit, highest)

    redge[...] = jnp.zeros_like(redge)
    lower = jnp.concatenate([jnp.zeros((HALF, CS), f32), rb[2, 0:HALF, :]], axis=0)
    redge[0, 2 * CS : 3 * CS, 0:HALF] = nn(ra[2], lower, highest)[:, HALF:CS]
    redge[1, 0:CS, 0:HALF] = ra[0, :, 0:HALF]
    for d in (0, 1):
        redge_t[d] = redge[d].T[0:HALF, :]
        xs[d] = nn(x, redge[d])
    rq_s[...] = rb[2][HALF:CS, HALF:CS]
    lq_s[...] = lb[5][HALF:CS, HALF:CS]

    for i in range(6):
        q[i * CS : (i + 1) * CS, :] = nn(la[i], g[i * CS : (i + 1) * CS, :])
    pbot[...] = nn(lb[5, HALF:CS, 0:HALF], q[HEIGHT - HALF : HEIGHT, :])
    qtop[...] = q[0:HALF, :]

    pl.semaphore_wait(barrier, len(peers))

    near = [
        remote(xs.at[0], x_in.at[0], xsem.at[0], xr.at[0], (r, cup)),
        remote(xs.at[1], x_in.at[1], xsem.at[1], xr.at[1], (r, cdn)),
        remote(rq_s, rq_in, cs.at[0], cr.at[0], (r, cup)),
        remote(lq_s, lq_in, cs.at[1], cr.at[1], (rup, c)),
        remote(pbot, pb_in.at[0], hs.at[0], hr.at[0], (rup, c)),
        remote(qtop, pb_in.at[1], hs.at[1], hr.at[1], (rdn, c)),
    ]
    for copy in near:
        copy.start()

    for i in range(5):
        y[HALF + i * CS : HALF + (i + 1) * CS, :] = nn(lb[i], q[HALF + i * CS : HALF + (i + 1) * CS, :])

    halos = []

    def send_edge(part):
        lo, hi = EDGE[part], EDGE[part + 1]
        for d, to in ((0, cup), (1, cdn)):
            edge[d, :, lo:hi] = nt(redge_t[d], y[lo:hi, :])
            copy = remote(
                edge.at[d, :, pl.ds(lo, hi - lo)], halo_out.at[d, :, pl.ds(lo, hi - lo)],
                es.at[d, part], er.at[d, part], (r, to),
            )
            copy.start()
            halos.append(copy)

    send_edge(1)
    for copy in near[3:]:
        copy.wait_recv()
    y[0:HALF, :] = pb_in[0] + nn(lq_in[...], q[0:HALF, :])
    y[HEIGHT - HALF : HEIGHT, :] = nn(lb[5, 0:HALF, :], jnp.concatenate([q[HEIGHT - HALF : HEIGHT, :], pb_in[1]], axis=0))
    send_edge(0)
    send_edge(2)

    ubuf[c, :, :] = jnp.zeros((KC, TALL), f32)
    ubuf[c, :, 0:HEIGHT] = nt(hit[48 : 48 + KC, :], y[...])
    u_far = remote(ubuf.at[c], ubuf.at[c], us.at[0], ur.at[0], far)
    u_far.start()

    wd[...] = jnp.zeros_like(wd)
    wd[0:HALF, 0:HALF] = jnp.where(iota((HALF, HALF), 0) == iota((HALF, HALF), 1), 1.0, 0.0)
    wd[HALF:CS, WIDTH - HALF : WIDTH] = rb[2, HALF:CS, 0:HALF]
    bloc[...] = jnp.zeros_like(bloc)
    bloc[HALF : HALF + CS, HALF : HALF + CS] = rb[0]
    bloc[HALF + CS : HALF + 2 * CS, HALF + CS : HALF + 2 * CS] = rb[1]
    bloc[WIDTH - HALF : WIDTH, WIDTH - HALF : WIDTH] = rb[2, 0:HALF, 0:HALF]
    near[2].wait_recv()
    bloc[0:HALF, 0:HALF] = rq_in[...]
    for i in range(3):
        rown[i * CS : (i + 1) * CS, :] = nn(ra[i], bloc[i * CS : (i + 1) * CS, :])

    near[0].wait_recv()
    near[1].wait_recv()
    right = nn(x, rown[...])
    for d in (0, 1):
        right += nn(x_in[d][:, 0:HALF], wd[d * HALF : (d + 1) * HALF, :])
    vbuf[r] = right + jnp.concatenate([jnp.zeros((KR, WIDE - 128), f32), piece], axis=1)

    def slot(j):
        return j * 2 + core

    def chain(j, way):
        to = {0: ((zl + 1) * 2 + core, c), 1: ((zl - 1) * 2 + core, c), 2: twin}[way]
        return remote(vbuf.at[slot(j)], vbuf.at[slot(j)], vs.at[way, j], vr.at[slot(j)], to)

    def arrival(s):
        return remote(vbuf.at[s], vbuf.at[s], vs.at[2, 0], vr.at[s], twin)

    def hand_on(j, way, act):
        go = zl < 7 if way == 0 else zl > 0

        @pl.when(go)
        def _():
            act(chain(j, way))

    start = lambda copy: copy.start()
    hand_on(zl, 0, start)
    hand_on(zl, 1, start)
    chain(zl, 2).start()

    def chain_step(s):
        for way, j, there in ((0, zl - s, zl - s >= 0), (1, zl + s, zl + s <= 7)):

            @pl.when(there)
            def _():
                arrival(slot(j)).wait_recv()
                hand_on(j, way, start)
                chain(j, 2).start()

    def chain_finish():
        for j in range(8):
            arrival(j * 2 + 1 - core).wait_recv()
        hand_on(zl, 0, lambda copy: copy.wait_send())
        hand_on(zl, 1, lambda copy: copy.wait_send())
        chain(zl, 2).wait_send()
        for s in range(1, 8):
            for way, j, there in ((0, zl - s, zl - s >= 0), (1, zl + s, zl + s <= 7)):

                @pl.when(there)
                def _():
                    hand_on(j, way, lambda copy: copy.wait_send())
                    chain(j, 2).wait_send()

    def spread(buf, first, count, send, recv, to):
        ref = buf.at[pl.ds(first, count)]
        return remote(ref, ref, send, recv, to)

    u_y = [spread(ubuf, xy * 2, 2, us.at[1 + d], ur.at[1 + d], ypeer[d]) for d in range(3)]
    u_x = [spread(ubuf, xx * 8, 8, us.at[4 + d], ur.at[4 + d], xpeer[d]) for d in range(3)]
    g_y = [spread(gbuf, xy * 2, 2, gs.at[1 + d], gr.at[1 + d], ypeer[d]) for d in range(3)]
    g_x = [spread(gbuf, xx * 8, 8, gs.at[4 + d], gr.at[4 + d], xpeer[d]) for d in range(3)]
    g_far = remote(gbuf.at[c], gbuf.at[c], gs.at[0], gr.at[0], far)

    u_y_in = [spread(ubuf, (xx * 4 + lax.rem(yy + 3 - d, 4)) * 2, 2, us.at[1 + d], ur.at[1 + d], ypeer[d]) for d in range(3)]
    u_x_in = [spread(ubuf, lax.rem(xx + 3 - d, 4) * 8, 8, us.at[4 + d], ur.at[4 + d], xpeer[d]) for d in range(3)]
    g_y_in = [spread(gbuf, (xx * 4 + lax.rem(yy + 3 - d, 4)) * 2, 2, gs.at[1 + d], gr.at[1 + d], ypeer[d]) for d in range(3)]
    g_x_in = [spread(gbuf, lax.rem(xx + 3 - d, 4) * 8, 8, gs.at[4 + d], gr.at[4 + d], xpeer[d]) for d in range(3)]
    u_far_in = remote(ubuf.at[c + 1 - 2 * zh], ubuf.at[c + 1 - 2 * zh], us.at[0], ur.at[0], far)
    g_far_in = remote(gbuf.at[c + 1 - 2 * zh], gbuf.at[c + 1 - 2 * zh], gs.at[0], gr.at[0], far)

    def rows_of_t(i):
        t[i * CS : (i + 1) * CS, :] = nn(y[i * CS : (i + 1) * CS, :], rown[...][:, 0:WIDTH])

    for s in range(1, 8):
        if s < 7:
            rows_of_t(s - 1)
        if s == 3:
            u_far_in.wait_recv()
            for copy in u_y:
                copy.start()
        if s == 5:
            for copy in u_y_in:
                copy.wait_recv()
            for copy in u_x:
                copy.start()
        chain_step(s)
    chain_finish()

    pieces = vbuf[...].reshape(K, WIDE)[:, WIDE - 128 :]
    gbuf[c] = pieces.T[48 : 48 + KC, :]
    g_far.start()
    outgoing = [pltpu.make_async_copy(t, t_out, outs.at[0]), pltpu.make_async_copy(vbuf, v_out, outs.at[1])]
    outgoing += [pltpu.make_async_copy(wd, wd_out, outs.at[2])]
    for copy in outgoing:
        copy.start()
    g_far_in.wait_recv()
    for copy in g_y:
        copy.start()
    for copy in g_y_in:
        copy.wait_recv()
    for copy in g_x:
        copy.start()
    for copy in u_x_in:
        copy.wait_recv()
    u[...] = ubuf[...].reshape(K, TALL).T
    outgoing.append(pltpu.make_async_copy(u, u_out, outs.at[3]))
    outgoing[-1].start()
    for copy in g_x_in:
        copy.wait_recv()
    gp[...] = gbuf[...].reshape(K, K).T
    outgoing.append(pltpu.make_async_copy(gp, gp_out, outs.at[4]))
    outgoing[-1].start()

    eye = iota((K, K), 0) == iota((K, K), 1)
    shifts = jnp.exp(-2.0 * coupling * field[...].astype(f32)) - 1.0
    pair = gp[...]
    diagonal = jnp.sum(jnp.where(eye, pair, 0.0), axis=0, keepdims=True)
    pivots = 1.0 + (1.0 - diagonal) * shifts
    ratio = shifts / pivots
    ratio_col = jnp.sum(jnp.where(eye, jnp.broadcast_to(ratio, (K, K)), 0.0), axis=1, keepdims=True)
    power = jnp.where(eye, 0.0, pair * ratio)
    z = vbuf[...].reshape(K, WIDE)[:, 0:WIDTH]
    for step in range(4):
        z = z + nn(power, z)
        if step < 3:
            power = nn(power, power)
    total = jnp.sum(jnp.sum(power * power, axis=1, keepdims=True), axis=0, keepdims=True)
    norm[...] = jnp.broadcast_to(total, norm.shape)
    outgoing.append(pltpu.make_async_copy(norm, norm_out, outs.at[5]))
    outgoing[-1].start()
    w = ratio_col * z
    for i in range(6):
        part = slice(i * CS, (i + 1) * CS)
        acc[part, :] = t[part, :] - nn(u[part, :], w)
    outgoing.append(pltpu.make_async_copy(acc, acc_out, outs.at[6]))
    outgoing[-1].start()

    for copy in outgoing:
        copy.wait()
    for copy in near:
        copy.wait_send()
    for copy in [u_far, g_far] + u_y + u_x + g_y + g_x:
        copy.wait_send()
    for copy in halos:
        copy.wait()


def finish_kernel(norm, field, acc, halo, wd, t_hbm, u_hbm, v_hbm, gp_hbm, out, t, u, v, gp, sem):
    edges = halo[...].reshape(2 * HALF, HEIGHT)
    out[...] = acc[...] + lax.dot_general(
        edges, wd[...], (((0,), (0,)), ((), ())), precision=high, preferred_element_type=f32
    )

    @pl.when(jnp.logical_not(norm[0, 0] < series_bound))
    def _():
        for i, (src, dst) in enumerate(((t_hbm, t), (u_hbm, u), (gp_hbm, gp))):
            copy = pltpu.make_async_copy(src, dst, sem.at[i])
            copy.start()
            copy.wait()
        copy = pltpu.make_async_copy(v_hbm, v, sem.at[3])
        copy.start()
        copy.wait()
        eye = iota((K, K), 0) == iota((K, K), 1)
        ident = jnp.where(eye, 1.0, 0.0)
        shifts = jnp.exp(-2.0 * coupling * field[...].astype(f32)) - 1.0
        gp[...] = ident + (ident - gp[...]) * shifts
        index = iota((K, 1), 0)

        def eliminate(k, carry):
            a = gp[...]
            column = jnp.sum(jnp.where(iota((K, K), 1) == k, a, 0.0), axis=1, keepdims=True)
            size = jnp.where(index >= k, jnp.abs(column), -1.0)
            best = jnp.min(jnp.where(size == jnp.max(size), index, K))
            at_k = jnp.sum(jnp.where(index == k, column, 0.0))
            at_best = jnp.sum(jnp.where(index == best, column, 0.0))
            factors = jnp.where(index == best, at_k, column)
            for ref in (gp, v):
                top = ref[pl.ds(best, 1), :] / at_best
                ref[pl.ds(best, 1), :] = ref[pl.ds(k, 1), :]
                ref[...] = jnp.where(index == k, top, ref[...] - factors * top)
            return carry

        lax.fori_loop(0, K, eliminate, 0)
        shift_col = jnp.sum(jnp.where(eye, jnp.broadcast_to(shifts, (K, K)), 0.0), axis=1, keepdims=True)
        w = shift_col * v[...][:, 0:WIDTH]
        fresh = t[...] - nn(u[...][0:HEIGHT, :], w, highest)
        out[...] = fresh + lax.dot_general(
            edges, wd[...], (((0,), (0,)), ((), ())), precision=high, preferred_element_type=f32
        )


def on_device(greens, accepted_sites, field_values, left_a, left_b, right_a, right_b):
    vmem = pl.BlockSpec(memory_space=pltpu.VMEM)
    smem = pl.BlockSpec(memory_space=pltpu.SMEM)
    hbm = pl.BlockSpec(memory_space=pl.ANY)
    shape = lambda *dims: jax.ShapeDtypeStruct(dims, f32)
    v = lambda *dims: pltpu.VMEM(dims, f32)
    dma = lambda *dims: pltpu.SemaphoreType.DMA(dims)
    field = field_values.reshape(1, K)
    acc, halo, wd, norm, t, u, vv, gp = pl.pallas_call(
        exchange_kernel,
        name="exchange",
        out_shape=[
            shape(HEIGHT, WIDTH), shape(2, HALF, HEIGHT), shape(2 * HALF, WIDE), shape(8, 128),
            shape(HEIGHT, WIDTH), shape(TALL, K), shape(ROWS, KR, WIDE), shape(K, K),
        ],
        in_specs=[smem] + [vmem] * 6,
        out_specs=[hbm] * 8,
        scratch_shapes=[
            v(HEIGHT, WIDTH), v(HEIGHT, WIDTH), v(HEIGHT, WIDTH), v(HEIGHT, WIDTH),
            v(HALF, WIDTH), v(HALF, WIDTH), v(2, HALF, WIDTH), v(HALF, HALF), v(HALF, HALF), v(HALF, HALF), v(HALF, HALF),
            v(2, WIDTH, 128), v(2, HALF, WIDTH), v(2 * HALF, WIDE), v(WIDTH, WIDE), v(WIDTH, WIDE),
            v(2, KR, 128), v(2, KR, 128), v(2, HALF, HEIGHT), v(COLS, KC, TALL), v(TALL, K), v(ROWS, KR, WIDE),
            v(COLS, KC, K), v(K, K), v(8, 128),
            dma(2, 3), dma(2, 3), dma(2), dma(2), dma(2), dma(2), dma(2), dma(2), dma(3, 8), dma(16),
            dma(7), dma(7), dma(7), dma(7), dma(7),
        ],
        compiler_params=pltpu.CompilerParams(collective_id=0, has_side_effects=True, vmem_limit_bytes=50 * 2**20),
    )(accepted_sites, field, greens, left_a, left_b, right_a, right_b)
    return pl.pallas_call(
        finish_kernel,
        name="finish",
        out_shape=shape(HEIGHT, WIDTH),
        in_specs=[smem] + [vmem] * 4 + [hbm] * 4,
        out_specs=vmem,
        scratch_shapes=[v(HEIGHT, WIDTH), v(TALL, K), v(K, WIDE), v(K, K), dma(4)],
        compiler_params=pltpu.CompilerParams(vmem_limit_bytes=50 * 2**20),
    )(norm, field, acc, halo, wd[:, 0:WIDTH], t, u, vv.reshape(K, WIDE), gp)


def solution(mesh):
    return jax.shard_map(
        on_device,
        mesh=mesh,
        in_specs=(
            P("row", "col"),
            P(),
            P(),
            P("row", None, None),
            P("row", None, None),
            P("col", None, None),
            P("col", None, None),
        ),
        out_specs=P("row", "col"),
        check_vma=False,
    )
```

```python
import jax
import jax.numpy as jnp
from jax import lax
from jax.experimental import pallas as pl
from jax.experimental.pallas import tpu as pltpu
from jax.sharding import PartitionSpec as P

MESH = pl.DeviceIdType.MESH
f32 = jnp.float32
high = lax.Precision.HIGH
highest = lax.Precision.HIGHEST
coupling = 0.45
series_bound = 1e-7

CS = 144
HALF = 72
ROWS, COLS = 16, 32
HEIGHT, WIDTH = 864, 432
K = 256
KR, KC = 16, 8
WIDE = 512
TALL = 896
BANDS = ((0, 256, 0, 512), (256, 512, 128, 768), (512, 768, 384, HEIGHT), (768, HEIGHT, 512, HEIGHT))
CHUNKS = 9


def dot(a, b, da, db, precision):
    return lax.dot_general(a, b, (((da,), (db,)), ((), ())), precision=precision, preferred_element_type=f32)


def nn(a, b, precision=high):
    return dot(a, b, 1, 0, precision)


def nt(a, b, precision=high):
    return dot(a, b, 1, 1, precision)


def tn(a, b, precision=high):
    return dot(a, b, 0, 0, precision)


def iota(shape, dim):
    return lax.broadcasted_iota(jnp.int32, shape, dim)


def exchange_kernel(
    sites, field, gt, la, lb, ra, rb,
    acc_out, halo_out, norm_out, t_out, u_out, v_out, gp_out,
    yt, tt, acc, ma, lf, rt, qtop, pbot, top_in, lq_s, lq_in, rq_s, rq_in, redge, redge_t, wd, bloc, rown, rown_t,
    xs, x_in, edge, pbuf, ubuf, vbuf, gbuf, gp, powers, ws, norm,
    es, er, ns, nr, ps, pr, vs, vr, us, ur, gs, gr, outs,
):
    r = lax.axis_index("row")
    c = lax.axis_index("col")
    zl, core = r // 2, lax.rem(r, 2)
    zh, xy = lax.rem(c, 2), c // 2
    yy, xx = lax.rem(xy, 4), xy // 4
    rup, rdn = lax.rem(r + 1, ROWS), lax.rem(r + ROWS - 1, ROWS)
    cup, cdn = lax.rem(c + 1, COLS), lax.rem(c + COLS - 1, COLS)
    twin = (r + 1 - 2 * core, c)
    far_c = c + 1 - 2 * zh
    mates = [(zl // 4) * 4 + lax.rem(lax.rem(zl, 4) + d, 4) for d in (1, 2, 3)]
    across = lax.rem(zl + 4, 8)
    on_line = lambda z: (z * 2 + core, c)
    ypeer = [(r, (xx * 4 + lax.rem(yy + d, 4)) * 2 + zh) for d in (1, 2, 3)]
    xpeer = [(r, (lax.rem(xx + d, 4) * 4 + yy) * 2 + zh) for d in (1, 2, 3)]
    peers = [(rup, c), (rdn, c), (r, cup), (r, cdn), on_line(across)] + [on_line(m) for m in mates] + ypeer + xpeer
    barrier = pltpu.get_barrier_semaphore()
    for peer in peers:
        pl.semaphore_signal(barrier, inc=1, device_id=peer, device_id_type=MESH)

    def remote(src, dst, send, recv, to):
        return pltpu.make_async_remote_copy(src, dst, send, recv, device_id=to, device_id_type=MESH)

    def begin(copies):
        for copy in copies:
            copy.start()

    def arrive(copies):
        for copy in copies:
            copy.wait_recv()

    lane = iota((1, 128), 1)
    row_site = jnp.full((1, 128), -1, jnp.int32)
    for j in range(KR):
        row_site = jnp.where(lane == j, sites[r * KR + j] - r * HEIGHT, row_site)
    rt[...] = nn(gt[...], jnp.where(iota((HEIGHT, 128), 0) == row_site, 1.0, 0.0))
    sub = iota((KR, WIDTH), 0)
    where_site = jnp.full((KR, WIDTH), -1, jnp.int32)
    for j in range(KR):
        where_site = jnp.where(sub == j, sites[r * KR + j] - c * WIDTH, where_site)
    x = jnp.where(iota((KR, WIDTH), 1) == where_site, 1.0, 0.0) - rt[...].T[0:KR, :]
    col_site = [jnp.clip(sites[c * KC + j] - c * WIDTH, 0, WIDTH - 1) for j in range(KC)]

    def site_rows(ref):
        shape = (KC, ref.shape[1])
        out = jnp.zeros(shape, f32)
        for j in range(KC):
            out = jnp.where(iota(shape, 0) == j, ref[pl.ds(col_site[j], 1), :], out)
        return out

    pbuf[r] = site_rows(rt)

    redge[...] = jnp.zeros_like(redge)
    lower = jnp.concatenate([jnp.zeros((HALF, CS), f32), rb[2, 0:HALF, :]], axis=0)
    redge[0, 2 * CS : 3 * CS, 0:HALF] = nn(ra[2], lower, highest)[:, HALF:CS]
    redge[1, 0:CS, 0:HALF] = ra[0, :, 0:HALF]
    for d in (0, 1):
        redge_t[d] = redge[d].T[0:HALF, :]
        xs[d] = nn(x, redge[d])
    rq_s[...] = rb[2][HALF:CS, HALF:CS]
    lq_s[...] = lb[5][HALF:CS, HALF:CS]

    ma[...] = jnp.zeros_like(ma)
    for i in range(6):
        ma[i * CS : (i + 1) * CS, i * CS : (i + 1) * CS] = la[i]
    qtop[...] = nt(gt[:, 0:CS], la[0, 0:HALF, :])
    last = nn(lb[5][HALF:CS, 0:HALF], ma[HEIGHT - HALF : HEIGHT, 640:TALL], highest)
    pbot[...] = nt(gt[:, 640:HEIGHT], last[:, 0 : HEIGHT - 640])

    pl.semaphore_wait(barrier, len(peers))

    near = [
        remote(pbot, top_in.at[0], ns.at[0], nr.at[0], (rup, c)),
        remote(qtop, top_in.at[1], ns.at[1], nr.at[1], (rdn, c)),
        remote(lq_s, lq_in, ns.at[2], nr.at[2], (rup, c)),
        remote(rq_s, rq_in, ns.at[3], nr.at[3], (r, cup)),
        remote(xs.at[0], x_in.at[0], ns.at[4], nr.at[4], (r, cup)),
        remote(xs.at[1], x_in.at[1], ns.at[5], nr.at[5], (r, cdn)),
    ]

    class Tree:
        def __init__(self, buf, send, recv):
            def go(z, i, to):
                ref = buf.at[z * 2 + core]
                return remote(ref, ref, send.at[i], recv.at[z * 2 + core], to)

            def come(s):
                return remote(buf.at[s], buf.at[s], send.at[0], recv.at[s], twin)

            self.first = [go(zl, d, on_line(mates[d])) for d in range(3)]
            self.first += [go(zl, 3, on_line(across)), go(zl, 4, twin)]
            self.across_in = come(across * 2 + core)
            self.second = [go(across, 5 + d, on_line(mates[d])) for d in range(3)] + [go(across, 8, twin)]
            self.mates_in = [come(m * 2 + core) for m in mates]
            self.mates_twin = [go(mates[d], 9 + d, twin) for d in range(3)]
            others = [lax.rem(m + 4, 8) for m in mates]
            self.others_in = [come(m * 2 + core) for m in others]
            self.others_twin = [go(others[d], 12 + d, twin) for d in range(3)]
            self.twins_in = [come(z * 2 + 1 - core) for z in range(8)]
            self.sent = self.first + self.second + self.mates_twin + self.others_twin

        def pass_across(self):
            self.across_in.wait_recv()
            begin(self.second)

        def pass_mates(self):
            for come, go in zip(self.mates_in, self.mates_twin):
                come.wait_recv()
                go.start()

        def pass_others(self):
            for come, go in zip(self.others_in, self.others_twin):
                come.wait_recv()
                go.start()

    p_tree, v_tree = Tree(pbuf, ps, pr), Tree(vbuf, vs, vr)
    begin(p_tree.first)
    begin(near)

    lf[...] = jnp.zeros_like(lf)
    for k in range(5):
        lo, hi = k * CS // 128 * 128, -(-(k + 2) * CS // 128) * 128
        band = slice(HALF + k * CS, HALF + (k + 1) * CS)
        lf[band, lo:hi] = nn(lb[k], ma[band, lo:hi], highest)
    lf[HEIGHT - HALF : HEIGHT, 640:TALL] = nn(lb[5][0:HALF, 0:HALF], ma[HEIGHT - HALF : HEIGHT, 640:TALL], highest)
    p_tree.pass_across()
    for a, b, lo, hi in BANDS:
        yt[:, a:b] = nt(gt[:, lo:hi], lf[a:b, lo:hi])
    p_tree.pass_mates()
    arrive(near[0:3])
    yt[:, 0:HALF] = top_in[0] + nt(qtop[...], lq_in[...])
    tail = jnp.concatenate([jnp.zeros((24, HALF), f32), lb[5][0:HALF, HALF:CS]], axis=0)
    yt[:, 768:HEIGHT] = yt[:, 768:HEIGHT] + nt(top_in[1], tail)
    p_tree.pass_others()

    edge[0] = nn(redge_t[0, :, 256:WIDTH], yt[256:WIDTH, :])
    edge[1] = nn(redge_t[1, :, 0:CS], yt[0:CS, :])
    halos = []
    for k in range(CHUNKS):
        part = pl.ds(k * 8, 8)
        for d, to in ((0, cup), (1, cdn)):
            halos.append(remote(edge.at[d, part], halo_out.at[d, part], es.at[d, k], er.at[d, k], (r, to)))
    poured = [0]

    def pour(n):
        begin(halos[poured[0] * 2 : (poured[0] + n) * 2])
        poured[0] = min(poured[0] + n, CHUNKS)

    class Spread:
        def __init__(self, buf, send, recv):
            def go(first, count, i, to):
                ref = buf.at[pl.ds(first, count)]
                return remote(ref, ref, send.at[i], recv.at[i], to)

            self.far = [go(c, 1, 0, (r, far_c))]
            self.far_in = [go(far_c, 1, 0, (r, far_c))]
            self.y = [go(xy * 2, 2, 1 + d, ypeer[d]) for d in range(3)]
            self.y_in = [go((xx * 4 + lax.rem(yy + 3 - d, 4)) * 2, 2, 1 + d, ypeer[d]) for d in range(3)]
            self.x = [go(xx * 8, 8, 4 + d, xpeer[d]) for d in range(3)]
            self.x_in = [go(lax.rem(xx + 3 - d, 4) * 8, 8, 4 + d, xpeer[d]) for d in range(3)]
            self.sent = self.far + self.y + self.x

    u_spread, g_spread = Spread(ubuf, us, ur), Spread(gbuf, gs, gr)
    ubuf[c] = site_rows(yt)
    begin(u_spread.far)
    pour(1)

    arrive(p_tree.twins_in)
    halves = []
    for h in (0, 1):
        half = pbuf[8 * h]
        for j in range(1, 8):
            half = half + pltpu.roll(pbuf[8 * h + j], 16 * j, 1)
        halves.append(half)
    gbuf[c] = jnp.concatenate(halves, axis=1)
    begin(g_spread.far)

    bloc[...] = jnp.zeros_like(bloc)
    bloc[HALF : HALF + CS, HALF : HALF + CS] = rb[0]
    bloc[HALF + CS : HALF + 2 * CS, HALF + CS : HALF + 2 * CS] = rb[1]
    bloc[WIDTH - HALF : WIDTH, WIDTH - HALF : WIDTH] = rb[2, 0:HALF, 0:HALF]
    wd[...] = jnp.zeros_like(wd)
    wd[:, WIDTH - HALF : WIDTH] = rb[2, HALF:CS, 0:HALF]
    near[3].wait_recv()
    bloc[0:HALF, 0:HALF] = rq_in[...]
    for i in range(3):
        rown[i * CS : (i + 1) * CS, :] = nn(ra[i], bloc[i * CS : (i + 1) * CS, :], highest)
    arrive(near[4:6])
    right = nn(x, rown[...]) + nn(x_in[1][:, 0:HALF], wd[...])
    vbuf[r] = right[:, 0:WIDTH] + jnp.concatenate([x_in[0], jnp.zeros((KR, WIDTH - 128), f32)], axis=1)
    begin(v_tree.first)
    pour(1)
    rown_t[...] = rown[...].T[0:WIDTH, :]

    def rows_of_t(i):
        part = slice(i * CS, (i + 1) * CS)
        tt[part, :] = nn(rown_t[part, :], yt[...])

    arrive(g_spread.far_in)
    begin(g_spread.y)
    v_tree.pass_across()
    arrive(u_spread.far_in)
    begin(u_spread.y)
    pour(1)
    rows_of_t(0)
    arrive(g_spread.y_in)
    begin(g_spread.x)
    v_tree.pass_mates()
    arrive(u_spread.y_in)
    begin(u_spread.x)
    pour(2)
    rows_of_t(1)
    v_tree.pass_others()
    pour(CHUNKS)
    rows_of_t(2)
    outgoing = [pltpu.make_async_copy(tt, t_out, outs.at[0])]
    outgoing[-1].start()

    arrive(g_spread.x_in)
    gp[...] = gbuf[...].reshape(K, K).T
    outgoing.append(pltpu.make_async_copy(gp, gp_out, outs.at[1]))
    outgoing[-1].start()
    eye = iota((K, K), 0) == iota((K, K), 1)
    shifts = jnp.exp(-2.0 * coupling * field[...].astype(f32)) - 1.0
    pair = gp[...]
    diagonal = jnp.sum(jnp.where(eye, pair, 0.0), axis=0, keepdims=True)
    ratio = shifts / (1.0 + (1.0 - diagonal) * shifts)
    ratio_col = jnp.sum(jnp.where(eye, jnp.broadcast_to(ratio, (K, K)), 0.0), axis=1, keepdims=True)
    powers[0] = jnp.where(eye, 0.0, pair * ratio)
    for step in range(3):
        powers[step + 1] = nn(powers[step], powers[step])
    total = jnp.sum(jnp.sum(powers[3] * powers[3], axis=1, keepdims=True), axis=0, keepdims=True)
    norm[...] = jnp.broadcast_to(total, norm.shape)
    outgoing.append(pltpu.make_async_copy(norm, norm_out, outs.at[2]))
    outgoing[-1].start()

    arrive(v_tree.twins_in)
    outgoing.append(pltpu.make_async_copy(vbuf, v_out, outs.at[3]))
    outgoing[-1].start()
    z = vbuf[...].reshape(K, WIDTH)
    for step in range(4):
        z = z + nn(powers[step], z)
    ws[...] = jnp.zeros_like(ws)
    ws[:, 0:WIDTH] = ratio_col * z
    wt = ws[...].T
    arrive(u_spread.x_in)
    outgoing.append(pltpu.make_async_copy(ubuf, u_out, outs.at[4]))
    outgoing[-1].start()
    for i in range(3):
        part = slice(i * CS, (i + 1) * CS)
        acc[part, :] = tt[part, :] - nn(wt[part, :], ubuf[...].reshape(K, HEIGHT))
    outgoing.append(pltpu.make_async_copy(acc, acc_out, outs.at[5]))
    outgoing[-1].start()

    for copy in outgoing:
        copy.wait()
    for copy in near + p_tree.sent + v_tree.sent + u_spread.sent + g_spread.sent:
        copy.wait_send()
    for copy in halos:
        copy.wait()


def finish_kernel(norm, field, halo, rb, acc_hbm, t_hbm, u_hbm, v_hbm, gp_hbm, out_hbm, low, top, t, u, v, gp, sem):
    inner = pl.ds(HALF, WIDTH - 2 * HALF)
    first, final = pl.ds(0, HALF), pl.ds(WIDTH - HALF, HALF)
    middle = pltpu.make_async_copy(acc_hbm.at[inner], out_hbm.at[inner], sem.at[0])
    loads = [pltpu.make_async_copy(acc_hbm.at[first], low, sem.at[1]), pltpu.make_async_copy(acc_hbm.at[final], top, sem.at[2])]
    stores = [pltpu.make_async_copy(low, out_hbm.at[first], sem.at[1]), pltpu.make_async_copy(top, out_hbm.at[final], sem.at[2])]
    middle.start()
    for copy in loads:
        copy.start()
    above = tn(rb[2][HALF:CS, 0:HALF], halo[1])
    loads[0].wait()
    low[...] = low[...] + halo[0]
    stores[0].start()
    loads[1].wait()
    top[...] = top[...] + above
    stores[1].start()
    middle.wait()
    for copy in stores:
        copy.wait()

    @pl.when(jnp.logical_not(norm[0, 0] < series_bound))
    def _():
        for i, (src, dst) in enumerate(((t_hbm, t), (u_hbm, u), (v_hbm, v), (gp_hbm, gp))):
            copy = pltpu.make_async_copy(src, dst, sem.at[i])
            copy.start()
            copy.wait()
        eye = iota((K, K), 0) == iota((K, K), 1)
        ident = jnp.where(eye, 1.0, 0.0)
        shifts = jnp.exp(-2.0 * coupling * field[...].astype(f32)) - 1.0
        gp[...] = ident + (ident - gp[...]) * shifts
        index = iota((K, 1), 0)

        def eliminate(k, carry):
            a = gp[...]
            column = jnp.sum(jnp.where(iota((K, K), 1) == k, a, 0.0), axis=1, keepdims=True)
            size = jnp.where(index >= k, jnp.abs(column), -1.0)
            best = jnp.min(jnp.where(size == jnp.max(size), index, K - 1))
            at_k = jnp.sum(jnp.where(index == k, column, 0.0))
            at_best = jnp.sum(jnp.where(index == best, column, 0.0))
            factors = jnp.where(index == best, at_k, column)
            for ref in (gp, v):
                line = ref[pl.ds(best, 1), :] / at_best
                ref[pl.ds(best, 1), :] = ref[pl.ds(k, 1), :]
                ref[...] = jnp.where(index == k, line, ref[...] - factors * line)
            return carry

        lax.fori_loop(0, K, eliminate, 0)
        shift_col = jnp.sum(jnp.where(eye, jnp.broadcast_to(shifts, (K, K)), 0.0), axis=1, keepdims=True)
        t[...] = t[...] - tn(shift_col * v[...], u[...], highest)
        t[0:HALF, :] = t[0:HALF, :] + halo[0]
        t[WIDTH - HALF : WIDTH, :] = t[WIDTH - HALF : WIDTH, :] + above
        copy = pltpu.make_async_copy(t, out_hbm, sem.at[0])
        copy.start()
        copy.wait()


def on_device(greens, accepted_sites, field_values, left_a, left_b, right_a, right_b):
    vmem = pl.BlockSpec(memory_space=pltpu.VMEM)
    smem = pl.BlockSpec(memory_space=pltpu.SMEM)
    hbm = pl.BlockSpec(memory_space=pltpu.HBM)
    shape = lambda *dims: jax.ShapeDtypeStruct(dims, f32)
    v = lambda *dims: pltpu.VMEM(dims, f32)
    dma = lambda *dims: pltpu.SemaphoreType.DMA(dims)
    field = field_values.reshape(1, K)
    acc, halo, norm, t, u, vv, gp = pl.pallas_call(
        exchange_kernel,
        name="exchange",
        out_shape=[
            shape(WIDTH, HEIGHT), shape(2, HALF, HEIGHT), shape(8, 128),
            shape(WIDTH, HEIGHT), shape(COLS, KC, HEIGHT), shape(ROWS, KR, WIDTH), shape(K, K),
        ],
        in_specs=[smem] + [vmem] * 6,
        out_specs=[hbm] * 7,
        scratch_shapes=[
            v(WIDTH, HEIGHT), v(WIDTH, HEIGHT), v(WIDTH, HEIGHT), v(HEIGHT, TALL), v(HEIGHT, TALL), v(WIDTH, 128),
            v(WIDTH, HALF), v(WIDTH, HALF), v(2, WIDTH, HALF), v(HALF, HALF), v(HALF, HALF), v(HALF, HALF), v(HALF, HALF),
            v(2, WIDTH, 128), v(2, HALF, WIDTH), v(HALF, WIDE), v(WIDTH, WIDE), v(WIDTH, WIDE), v(WIDTH, WIDTH),
            v(2, KR, 128), v(2, KR, 128), v(2, HALF, HEIGHT), v(ROWS, KC, 128), v(COLS, KC, HEIGHT), v(ROWS, KR, WIDTH),
            v(COLS, KC, K), v(K, K), v(4, K, K), v(K, WIDE), v(8, 128),
            dma(2, CHUNKS), dma(2, CHUNKS), dma(6), dma(6), dma(15), dma(16), dma(15), dma(16),
            dma(7), dma(7), dma(7), dma(7), dma(6),
        ],
        compiler_params=pltpu.CompilerParams(collective_id=0, has_side_effects=True, vmem_limit_bytes=50 * 2**20),
    )(accepted_sites, field, greens.T, left_a, left_b, right_a, right_b)
    out = pl.pallas_call(
        finish_kernel,
        name="finish",
        out_shape=shape(WIDTH, HEIGHT),
        in_specs=[smem] + [vmem] * 3 + [hbm] * 5,
        out_specs=hbm,
        scratch_shapes=[
            v(HALF, HEIGHT), v(HALF, HEIGHT), v(WIDTH, HEIGHT), v(K, HEIGHT), v(K, WIDTH), v(K, K), dma(4),
        ],
        compiler_params=pltpu.CompilerParams(vmem_limit_bytes=50 * 2**20),
    )(norm, field, halo, right_b, acc, t, u.reshape(K, HEIGHT), vv.reshape(K, WIDTH), gp)
    return out.T


def solution(mesh):
    return jax.shard_map(
        on_device,
        mesh=mesh,
        in_specs=(
            P("row", "col"),
            P(),
            P(),
            P("row", None, None),
            P("row", None, None),
            P("col", None, None),
            P("col", None, None),
        ),
        out_specs=P("row", "col"),
        check_vma=False,
    )
```

```python
import jax
import jax.numpy as jnp
from jax import lax
from jax.experimental import pallas as pl
from jax.experimental.pallas import tpu as pltpu
from jax.sharding import PartitionSpec as P

MESH = pl.DeviceIdType.MESH
f32 = jnp.float32
high = lax.Precision.HIGH
highest = lax.Precision.HIGHEST
coupling = 0.45
series_bound = 1e-7

CS = 144
HALF = 72
ROWS, COLS = 16, 32
HEIGHT, WIDTH = 864, 432
K = 256
KR, KC = 16, 8
WIDE = 512
TALL = 896
BANDS = ((0, 256, 0, 512), (256, 512, 128, 768), (512, 768, 384, HEIGHT), (768, HEIGHT, 512, HEIGHT))
CHUNKS = 9
POUR = (9, 0, 0, 9)


def dot(a, b, da, db, precision):
    return lax.dot_general(a, b, (((da,), (db,)), ((), ())), precision=precision, preferred_element_type=f32)


def nn(a, b, precision=high):
    return dot(a, b, 1, 0, precision)


def nt(a, b, precision=high):
    return dot(a, b, 1, 1, precision)


def tn(a, b, precision=high):
    return dot(a, b, 0, 0, precision)


def iota(shape, dim):
    return lax.broadcasted_iota(jnp.int32, shape, dim)


def exchange_kernel(
    sites_hbm, field_hbm, gt_hbm, la_hbm, lb_hbm, ra_hbm, rb_hbm,
    acc_out, halo_out, norm_out, mix_out, t_out, u_out, v_out, gp_out,
    sites, field, gt, la, lb, ra, rb, yt, tt, acc, ma, lf, rt, qtop, pbot, top_in, lq_s, lq_in, rq_s, rq_in, redge, redge_t, wd, bloc, rown, rown_t,
    xs, x_in, edge, pbuf, ubuf, vbuf, vall, gbuf, gp, powers, ws, norm, mix,
    es, er, ns, nr, ps, pr, vs, vr, us, ur, gs, gr, ins, outs,
):
    r = lax.axis_index("row")
    c = lax.axis_index("col")
    zl, core = r // 2, lax.rem(r, 2)
    zh, xy = lax.rem(c, 2), c // 2
    yy, xx = lax.rem(xy, 4), xy // 4
    rup, rdn = lax.rem(r + 1, ROWS), lax.rem(r + ROWS - 1, ROWS)
    cup, cdn = lax.rem(c + 1, COLS), lax.rem(c + COLS - 1, COLS)
    twin = (r + 1 - 2 * core, c)
    far_c = c + 1 - 2 * zh
    on_line = lambda z: (z * 2 + core, c)
    ypeer = [(r, (xx * 4 + lax.rem(yy + d, 4)) * 2 + zh) for d in (1, 2, 3)]
    xpeer = [(r, (lax.rem(xx + d, 4) * 4 + yy) * 2 + zh) for d in (1, 2, 3)]
    zf = zh * 8 + zl
    ring = [lax.rem(zf + d, 16) for d in range(1, 16)]
    on_ring = lambda z: (lax.rem(z, 8) * 2 + core, xy * 2 + z // 8)
    peers = [(rup, c), (rdn, c), (r, cup), (r, cdn)] + [on_ring(z) for z in ring] + ypeer + xpeer
    barrier = pltpu.get_barrier_semaphore()
    for peer in peers:
        pl.semaphore_signal(barrier, inc=1, device_id=peer, device_id_type=MESH)
    pairs = ((sites_hbm, sites), (gt_hbm, gt), (ra_hbm, ra), (rb_hbm, rb), (la_hbm, la), (lb_hbm, lb), (field_hbm, field))
    loads = [pltpu.make_async_copy(src, dst, ins.at[i]) for i, (src, dst) in enumerate(pairs)]
    for load in loads:
        load.start()
    redge[...] = jnp.zeros_like(redge)
    ma[...] = jnp.zeros_like(ma)
    lf[...] = jnp.zeros_like(lf)
    loads[0].wait()

    def remote(src, dst, send, recv, to):
        return pltpu.make_async_remote_copy(src, dst, send, recv, device_id=to, device_id_type=MESH)

    def begin(copies):
        for copy in copies:
            copy.start()

    def arrive(copies):
        for copy in copies:
            copy.wait_recv()

    lane = iota((1, 128), 1)
    row_site = jnp.full((1, 128), -1, jnp.int32)
    for j in range(KR):
        row_site = jnp.where(lane == j, sites[r * KR + j] - r * HEIGHT, row_site)
    loads[1].wait()
    rt[...] = nn(gt[...], jnp.where(iota((HEIGHT, 128), 0) == row_site, 1.0, 0.0))
    sub = iota((KR, WIDTH), 0)
    where_site = jnp.full((KR, WIDTH), -1, jnp.int32)
    for j in range(KR):
        where_site = jnp.where(sub == j, sites[r * KR + j] - c * WIDTH, where_site)
    x = jnp.where(iota((KR, WIDTH), 1) == where_site, 1.0, 0.0) - rt[...].T[0:KR, :]
    col_site = [jnp.clip(sites[c * KC + j] - c * WIDTH, 0, WIDTH - 1) for j in range(KC)]

    def site_rows(ref):
        shape = (KC, ref.shape[1])
        out = jnp.zeros(shape, f32)
        for j in range(KC):
            out = jnp.where(iota(shape, 0) == j, ref[pl.ds(col_site[j], 1), :], out)
        return out

    pbuf[core, zf] = site_rows(rt)

    loads[2].wait()
    loads[3].wait()
    lower = jnp.concatenate([jnp.zeros((HALF, CS), f32), rb[2, 0:HALF, :]], axis=0)
    redge[0, 2 * CS : 3 * CS, 0:HALF] = nn(ra[2], lower, highest)[:, HALF:CS]
    redge[1, 0:CS, 0:HALF] = ra[0, :, 0:HALF]
    for d in (0, 1):
        redge_t[d] = redge[d].T[0:HALF, :]
        xs[d] = nn(x, redge[d])
    rq_s[...] = rb[2][HALF:CS, HALF:CS]

    pl.semaphore_wait(barrier, len(peers))

    far = [
        remote(xs.at[0], x_in.at[0], ns.at[4], nr.at[4], (r, cup)),
        remote(xs.at[1], x_in.at[1], ns.at[5], nr.at[5], (r, cdn)),
        remote(rq_s, rq_in, ns.at[3], nr.at[3], (r, cup)),
    ]
    begin(far)
    pieces = [remote(pbuf.at[core, zf], pbuf.at[core, zf], ps.at[d], pr.at[zf], on_ring(ring[d])) for d in range(15)]
    pieces_in = [remote(pbuf.at[core, z], pbuf.at[core, z], ps.at[0], pr.at[z], twin) for z in ring]
    pieces_twin = remote(pbuf.at[core], pbuf.at[core], ps.at[15], pr.at[16], twin)
    pieces_twin_in = remote(pbuf.at[1 - core], pbuf.at[1 - core], ps.at[15], pr.at[16], twin)
    begin(pieces)

    mix[...] = rb[2][HALF:CS, 0:HALF]
    outgoing = [pltpu.make_async_copy(mix, mix_out, outs.at[8])]
    outgoing[-1].start()
    loads[4].wait()
    loads[5].wait()
    loads[6].wait()
    lq_s[...] = lb[5][HALF:CS, HALF:CS]

    for i in range(6):
        ma[i * CS : (i + 1) * CS, i * CS : (i + 1) * CS] = la[i]
    qtop[...] = nt(la[0, 0:HALF, :], gt[:, 0:CS])
    last = nn(lb[5][HALF:CS, 0:HALF], ma[HEIGHT - HALF : HEIGHT, 640:TALL], highest)
    pbot[...] = nt(last[:, 0 : HEIGHT - 640], gt[:, 640:HEIGHT])

    near = [
        remote(pbot, top_in.at[0], ns.at[0], nr.at[0], (rup, c)),
        remote(qtop, top_in.at[1], ns.at[1], nr.at[1], (rdn, c)),
        remote(lq_s, lq_in, ns.at[2], nr.at[2], (rup, c)),
    ]
    begin(near)

    others = [lax.rem(zl + d, 8) for d in range(1, 8)]
    rows_out = [remote(vbuf.at[core, zl], vbuf.at[core, zl], vs.at[d], vr.at[zl], on_line(others[d])) for d in range(7)]
    rows_in = [remote(vbuf.at[core, z], vbuf.at[core, z], vs.at[0], vr.at[z], twin) for z in others]
    rows_twin = remote(vbuf.at[core], vbuf.at[core], vs.at[7], vr.at[8], twin)
    rows_twin_in = remote(vbuf.at[1 - core], vbuf.at[1 - core], vs.at[7], vr.at[8], twin)

    for k in range(5):
        lo, hi = k * CS // 128 * 128, -(-(k + 2) * CS // 128) * 128
        band = slice(HALF + k * CS, HALF + (k + 1) * CS)
        lf[band, lo:hi] = nn(lb[k], ma[band, lo:hi], highest)
    lf[HEIGHT - HALF : HEIGHT, 640:TALL] = nn(lb[5][0:HALF, 0:HALF], ma[HEIGHT - HALF : HEIGHT, 640:TALL], highest)
    bloc[...] = jnp.zeros_like(bloc)
    bloc[HALF : HALF + CS, HALF : HALF + CS] = rb[0]
    bloc[HALF + CS : HALF + 2 * CS, HALF + CS : HALF + 2 * CS] = rb[1]
    bloc[WIDTH - HALF : WIDTH, WIDTH - HALF : WIDTH] = rb[2, 0:HALF, 0:HALF]
    wd[...] = jnp.zeros_like(wd)
    wd[:, WIDTH - HALF : WIDTH] = rb[2, HALF:CS, 0:HALF]
    for i in range(3):
        rown[i * CS : (i + 1) * CS, :] = nn(ra[i], bloc[i * CS : (i + 1) * CS, :], highest)
    right = nn(x, rown[...])
    for a, b, lo, hi in BANDS:
        yt[:, a:b] = nt(gt[:, lo:hi], lf[a:b, lo:hi])
    arrive(far)
    first = x_in[0] + jnp.concatenate([nn(xs[1][:, 0:HALF], rq_in[...]), jnp.zeros((KR, 128 - HALF), f32)], axis=1)
    right += nn(x_in[1][:, 0:HALF], wd[...])
    vbuf[core, zl] = right[:, 0:WIDTH] + jnp.concatenate([first, jnp.zeros((KR, WIDTH - 128), f32)], axis=1)
    begin(rows_out)
    arrive(near)
    one = jnp.where(iota((HALF, HALF), 0) == iota((HALF, HALF), 1), 1.0, 0.0)
    yt[:, 0:HALF] = tn(jnp.concatenate([top_in[0], nn(lq_in[...], qtop[...])], axis=0), jnp.concatenate([one, one], axis=0))
    tail = jnp.concatenate([jnp.zeros((24, HALF), f32), lb[5][0:HALF, HALF:CS]], axis=0)
    yt[:, 768:HEIGHT] = yt[:, 768:HEIGHT] + tn(top_in[1], tail.T)

    edge[0] = nn(redge_t[0, :, 256:WIDTH], yt[256:WIDTH, :])
    edge[1] = nn(redge_t[1, :, 0:CS], yt[0:CS, :])
    halos = []
    for k in range(CHUNKS):
        part = pl.ds(k * 8, 8)
        for d, to in ((0, cup), (1, cdn)):
            halos.append(remote(edge.at[d, part], halo_out.at[d, part], es.at[d, k], er.at[d, k], (r, to)))
    poured = [0]

    def pour(n):
        begin(halos[poured[0] * 2 : (poured[0] + n) * 2])
        poured[0] = min(poured[0] + n, CHUNKS)

    class Spread:
        def __init__(self, buf, send, recv):
            def go(first, count, i, to):
                ref = buf.at[pl.ds(first, count)]
                return remote(ref, ref, send.at[i], recv.at[i], to)

            self.far = [go(c, 1, 0, (r, far_c))]
            self.far_in = [go(far_c, 1, 0, (r, far_c))]
            self.y = [go(xy * 2, 2, 1 + d, ypeer[d]) for d in range(3)]
            self.y_in = [go((xx * 4 + lax.rem(yy + 3 - d, 4)) * 2, 2, 1 + d, ypeer[d]) for d in range(3)]
            self.x = [go(xx * 8, 8, 4 + d, xpeer[d]) for d in range(3)]
            self.x_in = [go(lax.rem(xx + 3 - d, 4) * 8, 8, 4 + d, xpeer[d]) for d in range(3)]
            self.sent = self.far + self.y + self.x

    u_spread, g_spread = Spread(ubuf, us, ur), Spread(gbuf, gs, gr)
    ubuf[c] = site_rows(yt)
    begin(u_spread.far)
    pour(POUR[0])

    arrive(pieces_in)
    pieces_twin.start()
    pour(POUR[1])
    pieces_twin_in.wait_recv()
    for side in (0, 1):
        halves = []
        for h in (0, 1):
            half = pbuf[0, side * 8 + 4 * h]
            for j in range(1, 8):
                half = half + pltpu.roll(pbuf[j % 2, side * 8 + 4 * h + j // 2], 16 * j, 1)
            halves.append(half)
        gbuf[xy * 2 + side] = jnp.concatenate(halves, axis=1)
    begin(g_spread.y)
    pour(POUR[2])
    rown_t[...] = rown[...].T[0:WIDTH, :]

    def rows_of_t(i):
        part = slice(i * CS, (i + 1) * CS)
        tt[part, :] = nn(rown_t[part, :], yt[...])

    arrive(g_spread.y_in)
    begin(g_spread.x)
    pour(POUR[3])
    rows_of_t(0)
    tt[0:HALF, :] = tt[0:HALF, :] + tn(rq_in[...], edge[1])
    arrive(u_spread.far_in)
    begin(u_spread.y)
    rows_of_t(1)
    rows_of_t(2)
    outgoing.append(pltpu.make_async_copy(tt, t_out, outs.at[0]))
    outgoing[-1].start()

    arrive(g_spread.x_in)
    gp[...] = gbuf[...].reshape(K, K).T
    outgoing.append(pltpu.make_async_copy(gp, gp_out, outs.at[1]))
    outgoing[-1].start()
    eye = iota((K, K), 0) == iota((K, K), 1)
    shifts = jnp.exp(-2.0 * coupling * field[...].astype(f32)) - 1.0
    pair = gp[...]
    diagonal = jnp.sum(jnp.where(eye, pair, 0.0), axis=0, keepdims=True)
    ratio = shifts / (1.0 + (1.0 - diagonal) * shifts)
    ratio_col = jnp.sum(jnp.where(eye, jnp.broadcast_to(ratio, (K, K)), 0.0), axis=1, keepdims=True)
    powers[0] = jnp.where(eye, 0.0, pair * ratio)
    for step in range(3):
        powers[step + 1] = nn(powers[step], powers[step])
    arrive(u_spread.y_in)
    begin(u_spread.x)
    arrive(rows_in)
    rows_twin.start()
    total = jnp.sum(jnp.sum(powers[3] * powers[3], axis=1, keepdims=True), axis=0, keepdims=True)
    norm[...] = jnp.broadcast_to(total, norm.shape)
    outgoing.append(pltpu.make_async_copy(norm, norm_out, outs.at[2]))
    outgoing[-1].start()

    rows_twin_in.wait_recv()
    for k in range(ROWS):
        vall[k * KR : (k + 1) * KR, :] = vbuf[k % 2, k // 2]
    outgoing.append(pltpu.make_async_copy(vall, v_out, outs.at[3]))
    outgoing[-1].start()
    z = vall[...]
    for step in range(4):
        z = z + nn(powers[step], z)
    ws[...] = jnp.zeros_like(ws)
    ws[:, 0:WIDTH] = ratio_col * z
    wt = ws[...].T
    arrive(u_spread.x_in)
    outgoing.append(pltpu.make_async_copy(ubuf, u_out, outs.at[4]))
    outgoing[-1].start()
    for i in range(3):
        part = slice(i * CS, (i + 1) * CS)
        acc[part, :] = tt[part, :] - nn(wt[part, :], ubuf[...].reshape(K, HEIGHT))
        outgoing.append(pltpu.make_async_copy(acc.at[part], acc_out.at[part], outs.at[5 + i]))
        outgoing[-1].start()

    for copy in outgoing:
        copy.wait()
    for copy in near + far + pieces + [pieces_twin] + rows_out + [rows_twin] + u_spread.sent + g_spread.y + g_spread.x:
        copy.wait_send()
    for copy in halos:
        copy.wait()


def finish_kernel(norm_hbm, acc_hbm, halo_hbm, mix_hbm, field_hbm, t_hbm, u_hbm, v_hbm, gp_hbm, out_hbm, norm, acc, halo, mix, field, t, u, v, gp, sem, out_sem):
    first, inner, final = pl.ds(0, HALF), pl.ds(HALF, WIDTH - 2 * HALF), pl.ds(WIDTH - HALF, HALF)
    pairs = [(halo_hbm, halo), (mix_hbm, mix)] + [(acc_hbm.at[part], acc.at[part]) for part in (final, first, inner)]
    pairs.append((norm_hbm, norm))
    loads = [pltpu.make_async_copy(src, dst, sem.at[i]) for i, (src, dst) in enumerate(pairs)]
    stores = [pltpu.make_async_copy(acc.at[part], out_hbm.at[part], out_sem.at[i]) for i, part in enumerate((final, first, inner))]
    for load in loads:
        load.start()
    loads[0].wait()
    loads[1].wait()
    above = tn(mix[...], halo[1])
    loads[2].wait()
    acc[WIDTH - HALF : WIDTH, :] = acc[WIDTH - HALF : WIDTH, :] + above
    stores[0].start()
    loads[3].wait()
    acc[0:HALF, :] = acc[0:HALF, :] + halo[0]
    stores[1].start()
    loads[4].wait()
    stores[2].start()
    loads[5].wait()
    for copy in stores:
        copy.wait()

    @pl.when(jnp.logical_not(norm[0, 0] < series_bound))
    def _():
        for i, (src, dst) in enumerate(((t_hbm, t), (u_hbm, u), (v_hbm, v), (gp_hbm, gp), (field_hbm, field))):
            copy = pltpu.make_async_copy(src, dst, sem.at[i])
            copy.start()
            copy.wait()
        eye = iota((K, K), 0) == iota((K, K), 1)
        ident = jnp.where(eye, 1.0, 0.0)
        shifts = jnp.exp(-2.0 * coupling * field[...].astype(f32)) - 1.0
        gp[...] = ident + (ident - gp[...]) * shifts
        index = iota((K, 1), 0)

        def eliminate(k, carry):
            a = gp[...]
            column = jnp.sum(jnp.where(iota((K, K), 1) == k, a, 0.0), axis=1, keepdims=True)
            size = jnp.where(index >= k, jnp.abs(column), -1.0)
            best = jnp.min(jnp.where(size == jnp.max(size), index, K - 1))
            at_k = jnp.sum(jnp.where(index == k, column, 0.0))
            at_best = jnp.sum(jnp.where(index == best, column, 0.0))
            factors = jnp.where(index == best, at_k, column)
            for ref in (gp, v):
                line = ref[pl.ds(best, 1), :] / at_best
                ref[pl.ds(best, 1), :] = ref[pl.ds(k, 1), :]
                ref[...] = jnp.where(index == k, line, ref[...] - factors * line)
            return carry

        lax.fori_loop(0, K, eliminate, 0)
        shift_col = jnp.sum(jnp.where(eye, jnp.broadcast_to(shifts, (K, K)), 0.0), axis=1, keepdims=True)
        t[...] = t[...] - tn(shift_col * v[...], u[...], highest)
        t[0:HALF, :] = t[0:HALF, :] + halo[0]
        t[WIDTH - HALF : WIDTH, :] = t[WIDTH - HALF : WIDTH, :] + above
        copy = pltpu.make_async_copy(t, out_hbm, sem.at[0])
        copy.start()
        copy.wait()


def on_device(greens, accepted_sites, field_values, left_a, left_b, right_a, right_b):
    hbm = pl.BlockSpec(memory_space=pltpu.HBM)
    shape = lambda *dims: jax.ShapeDtypeStruct(dims, f32)
    v = lambda *dims: pltpu.VMEM(dims, f32)
    dma = lambda *dims: pltpu.SemaphoreType.DMA(dims)
    smem_v = lambda *dims: pltpu.SMEM(dims, jnp.int32)
    field = field_values.reshape(1, K)
    acc, halo, norm, mix, t, u, vv, gp = pl.pallas_call(
        exchange_kernel,
        name="exchange",
        out_shape=[
            shape(WIDTH, HEIGHT), shape(2, HALF, HEIGHT), shape(8, 128), shape(HALF, HALF),
            shape(WIDTH, HEIGHT), shape(COLS, KC, HEIGHT), shape(K, WIDTH), shape(K, K),
        ],
        in_specs=[hbm] * 7,
        out_specs=[hbm] * 8,
        scratch_shapes=[
            smem_v(K), pltpu.VMEM((1, K), jnp.int32), v(WIDTH, HEIGHT), v(6, CS, CS), v(6, CS, CS), v(3, CS, CS), v(3, CS, CS),
            v(WIDTH, HEIGHT), v(WIDTH, HEIGHT), v(WIDTH, HEIGHT), v(HEIGHT, TALL), v(HEIGHT, TALL), v(WIDTH, 128),
            v(HALF, WIDTH), v(HALF, WIDTH), v(2, HALF, WIDTH), v(HALF, HALF), v(HALF, HALF), v(HALF, HALF), v(HALF, HALF),
            v(2, WIDTH, 128), v(2, HALF, WIDTH), v(HALF, WIDE), v(WIDTH, WIDE), v(WIDTH, WIDE), v(WIDTH, WIDTH),
            v(2, KR, 128), v(2, KR, 128), v(2, HALF, HEIGHT), v(2, ROWS, KC, 128), v(COLS, KC, HEIGHT), v(2, 8, KR, WIDTH), v(K, WIDTH),
            v(COLS, KC, K), v(K, K), v(4, K, K), v(K, WIDE), v(8, 128), v(HALF, HALF),
            dma(2, CHUNKS), dma(2, CHUNKS), dma(6), dma(6), dma(16), dma(17), dma(8), dma(9),
            dma(7), dma(7), dma(7), dma(7), dma(7), dma(9),
        ],
        compiler_params=pltpu.CompilerParams(collective_id=0, has_side_effects=True, vmem_limit_bytes=60 * 2**20),
    )(accepted_sites, field, greens.T, left_a, left_b, right_a, right_b)
    out = pl.pallas_call(
        finish_kernel,
        name="finish",
        out_shape=shape(WIDTH, HEIGHT),
        in_specs=[hbm] * 9,
        out_specs=hbm,
        scratch_shapes=[
            pltpu.SMEM((8, 128), f32), v(WIDTH, HEIGHT), v(2, HALF, HEIGHT), v(HALF, HALF), pltpu.VMEM((1, K), jnp.int32),
            v(WIDTH, HEIGHT), v(K, HEIGHT), v(K, WIDTH), v(K, K), dma(6), dma(3),
        ],
        compiler_params=pltpu.CompilerParams(vmem_limit_bytes=60 * 2**20),
    )(norm, acc, halo, mix, field, t, u.reshape(K, HEIGHT), vv, gp)
    return out.T


def solution(mesh):
    return jax.shard_map(
        on_device,
        mesh=mesh,
        in_specs=(
            P("row", "col"),
            P(),
            P(),
            P("row", None, None),
            P("row", None, None),
            P("col", None, None),
            P("col", None, None),
        ),
        out_specs=P("row", "col"),
        check_vma=False,
    )
```

```python
import jax
import jax.numpy as jnp
from jax import lax
from jax.experimental import pallas as pl
from jax.experimental.pallas import tpu as pltpu
from jax.sharding import PartitionSpec as P

MESH = pl.DeviceIdType.MESH
f32 = jnp.float32
high = lax.Precision.HIGH
highest = lax.Precision.HIGHEST
coupling = 0.45
series_bound = 1e-7

CS = 144
HALF = 72
ROWS, COLS = 16, 32
HEIGHT, WIDTH = 864, 432
K = 256
KR, KC = 16, 8
WIDE = 512
TALL = 896
BANDS = ((0, 256, 0, 512), (256, 512, 128, 768), (512, 768, 384, HEIGHT), (768, HEIGHT, 512, HEIGHT))


def dot(a, b, da, db, precision):
    return lax.dot_general(a, b, (((da,), (db,)), ((), ())), precision=precision, preferred_element_type=f32)


def nn(a, b, precision=high):
    return dot(a, b, 1, 0, precision)


def nt(a, b, precision=high):
    return dot(a, b, 1, 1, precision)


def tn(a, b, precision=high):
    return dot(a, b, 0, 0, precision)


def iota(shape, dim):
    return lax.broadcasted_iota(jnp.int32, shape, dim)


def exchange_kernel(
    sites_hbm, field_hbm, gt_hbm, la_hbm, lb_hbm, ra_hbm, rb_hbm,
    acc_out, halo_out, norm_out, mix_out, t_out, u_out, v_out, gp_out,
    sites, field, gt, la, lb, ra, rb, yt, tt, acc, ma, lf, rt, qtop, pbot, top_in, lq_s, lq_in, rq_s, rq_in, redge, redge_t, wd, bloc, rown, rown_t,
    xs, x_in, edge, pbuf, ubuf, vbuf, vall, gbuf, gp, powers, ws, norm, mix,
    es, er, ns, nr, ps, pr, vs, vr, us, ur, gs, gr, ins, outs,
):
    r = lax.axis_index("row")
    c = lax.axis_index("col")
    zl, core = r // 2, lax.rem(r, 2)
    zh, xy = lax.rem(c, 2), c // 2
    yy, xx = lax.rem(xy, 4), xy // 4
    rup, rdn = lax.rem(r + 1, ROWS), lax.rem(r + ROWS - 1, ROWS)
    cup, cdn = lax.rem(c + 1, COLS), lax.rem(c + COLS - 1, COLS)
    twin = (r + 1 - 2 * core, c)
    far_c = c + 1 - 2 * zh
    on_line = lambda z: (z * 2 + core, c)
    ypeer = [(r, (xx * 4 + lax.rem(yy + d, 4)) * 2 + zh) for d in (1, 2, 3)]
    xpeer = [(r, (lax.rem(xx + d, 4) * 4 + yy) * 2 + zh) for d in (1, 2, 3)]
    zf = zh * 8 + zl
    ring = [lax.rem(zf + d, 16) for d in range(1, 16)]
    on_ring = lambda z: (lax.rem(z, 8) * 2 + core, xy * 2 + z // 8)
    peers = [(rup, c), (rdn, c), (r, cup), (r, cdn)] + [on_ring(z) for z in ring] + ypeer + xpeer
    barrier = pltpu.get_barrier_semaphore()
    for peer in peers:
        pl.semaphore_signal(barrier, inc=1, device_id=peer, device_id_type=MESH)
    pairs = ((sites_hbm, sites), (gt_hbm, gt), (ra_hbm, ra), (rb_hbm, rb), (la_hbm, la), (lb_hbm, lb), (field_hbm, field))
    loads = [pltpu.make_async_copy(src, dst, ins.at[i]) for i, (src, dst) in enumerate(pairs)]
    for load in loads:
        load.start()
    redge[...] = jnp.zeros_like(redge)
    ma[...] = jnp.zeros_like(ma)
    lf[...] = jnp.zeros_like(lf)
    loads[0].wait()

    def remote(src, dst, send, recv, to):
        return pltpu.make_async_remote_copy(src, dst, send, recv, device_id=to, device_id_type=MESH)

    def begin(copies):
        for copy in copies:
            copy.start()

    def arrive(copies):
        for copy in copies:
            copy.wait_recv()

    lane = iota((1, 128), 1)
    row_site = jnp.full((1, 128), -1, jnp.int32)
    for j in range(KR):
        row_site = jnp.where(lane == j, sites[r * KR + j] - r * HEIGHT, row_site)
    loads[1].wait()
    rt[...] = nn(gt[...], jnp.where(iota((HEIGHT, 128), 0) == row_site, 1.0, 0.0))
    sub = iota((KR, WIDTH), 0)
    where_site = jnp.full((KR, WIDTH), -1, jnp.int32)
    for j in range(KR):
        where_site = jnp.where(sub == j, sites[r * KR + j] - c * WIDTH, where_site)
    x = jnp.where(iota((KR, WIDTH), 1) == where_site, 1.0, 0.0) - rt[...].T[0:KR, :]
    col_site = [jnp.clip(sites[c * KC + j] - c * WIDTH, 0, WIDTH - 1) for j in range(KC)]

    def site_rows(ref):
        shape = (KC, ref.shape[1])
        out = jnp.zeros(shape, f32)
        for j in range(KC):
            out = jnp.where(iota(shape, 0) == j, ref[pl.ds(col_site[j], 1), :], out)
        return out

    pbuf[core, zf] = site_rows(rt)

    loads[2].wait()
    loads[3].wait()
    lower = jnp.concatenate([jnp.zeros((HALF, CS), f32), rb[2, 0:HALF, :]], axis=0)
    redge[0, 2 * CS : 3 * CS, 0:HALF] = nn(ra[2], lower, highest)[:, HALF:CS]
    redge[1, 0:CS, 0:HALF] = ra[0, :, 0:HALF]
    for d in (0, 1):
        redge_t[d] = redge[d].T[0:HALF, :]
        xs[d] = nn(x, redge[d])
    rq_s[...] = rb[2][HALF:CS, HALF:CS]

    pl.semaphore_wait(barrier, len(peers))

    far = [
        remote(xs.at[0], x_in.at[0], ns.at[4], nr.at[4], (r, cup)),
        remote(xs.at[1], x_in.at[1], ns.at[5], nr.at[5], (r, cdn)),
        remote(rq_s, rq_in, ns.at[3], nr.at[3], (r, cup)),
    ]
    begin(far)
    pieces = [remote(pbuf.at[core, zf], pbuf.at[core, zf], ps.at[d], pr.at[zf], on_ring(ring[d])) for d in range(15)]
    pieces_in = [remote(pbuf.at[core, z], pbuf.at[core, z], ps.at[0], pr.at[z], twin) for z in ring]
    pieces_twin = remote(pbuf.at[core], pbuf.at[core], ps.at[15], pr.at[16], twin)
    pieces_twin_in = remote(pbuf.at[1 - core], pbuf.at[1 - core], ps.at[15], pr.at[16], twin)
    begin(pieces)

    mix[...] = rb[2][HALF:CS, 0:HALF]
    outgoing = [pltpu.make_async_copy(mix, mix_out, outs.at[8])]
    outgoing[-1].start()
    loads[4].wait()
    loads[5].wait()
    loads[6].wait()
    lq_s[...] = lb[5][HALF:CS, HALF:CS]

    for i in range(6):
        ma[i * CS : (i + 1) * CS, i * CS : (i + 1) * CS] = la[i]
    qtop[...] = nt(la[0, 0:HALF, :], gt[:, 0:CS])
    last = nn(lb[5][HALF:CS, 0:HALF], ma[HEIGHT - HALF : HEIGHT, 640:TALL], highest)
    pbot[...] = nt(last[:, 0 : HEIGHT - 640], gt[:, 640:HEIGHT])

    near = [
        remote(pbot, top_in.at[0], ns.at[0], nr.at[0], (rup, c)),
        remote(qtop, top_in.at[1], ns.at[1], nr.at[1], (rdn, c)),
        remote(lq_s, lq_in, ns.at[2], nr.at[2], (rup, c)),
    ]
    begin(near)

    others = [lax.rem(zl + d, 8) for d in range(1, 8)]
    rows_out = [remote(vbuf.at[core, zl], vbuf.at[core, zl], vs.at[d], vr.at[zl], on_line(others[d])) for d in range(7)]
    rows_in = [remote(vbuf.at[core, z], vbuf.at[core, z], vs.at[0], vr.at[z], twin) for z in others]
    rows_twin = remote(vbuf.at[core], vbuf.at[core], vs.at[7], vr.at[8], twin)
    rows_twin_in = remote(vbuf.at[1 - core], vbuf.at[1 - core], vs.at[7], vr.at[8], twin)

    for k in range(5):
        lo, hi = k * CS // 128 * 128, -(-(k + 2) * CS // 128) * 128
        band = slice(HALF + k * CS, HALF + (k + 1) * CS)
        lf[band, lo:hi] = nn(lb[k], ma[band, lo:hi], highest)
    lf[HEIGHT - HALF : HEIGHT, 640:TALL] = nn(lb[5][0:HALF, 0:HALF], ma[HEIGHT - HALF : HEIGHT, 640:TALL], highest)
    bloc[...] = jnp.zeros_like(bloc)
    bloc[HALF : HALF + CS, HALF : HALF + CS] = rb[0]
    bloc[HALF + CS : HALF + 2 * CS, HALF + CS : HALF + 2 * CS] = rb[1]
    bloc[WIDTH - HALF : WIDTH, WIDTH - HALF : WIDTH] = rb[2, 0:HALF, 0:HALF]
    wd[...] = jnp.zeros_like(wd)
    wd[:, WIDTH - HALF : WIDTH] = rb[2, HALF:CS, 0:HALF]
    for i in range(3):
        rown[i * CS : (i + 1) * CS, :] = nn(ra[i], bloc[i * CS : (i + 1) * CS, :], highest)
    right = nn(x, rown[...])
    for a, b, lo, hi in BANDS:
        yt[:, a:b] = nt(gt[:, lo:hi], lf[a:b, lo:hi])
    arrive(far[0:2])
    right += nn(x_in[1][:, 0:HALF], wd[...])
    vbuf[core, zl] = right + jnp.concatenate([x_in[0], jnp.zeros((KR, 256), f32), pltpu.roll(xs[1], 48, 1)], axis=1)
    begin(rows_out)
    arrive(near)
    one = jnp.where(iota((HALF, HALF), 0) == iota((HALF, HALF), 1), 1.0, 0.0)
    yt[:, 0:HALF] = tn(jnp.concatenate([top_in[0], nn(lq_in[...], qtop[...])], axis=0), jnp.concatenate([one, one], axis=0))
    tail = jnp.concatenate([jnp.zeros((24, HALF), f32), lb[5][0:HALF, HALF:CS]], axis=0)
    yt[:, 768:HEIGHT] = yt[:, 768:HEIGHT] + tn(top_in[1], tail.T)

    edge[0] = nn(redge_t[0, :, 256:WIDTH], yt[256:WIDTH, :])
    edge[1] = nn(redge_t[1, :, 0:CS], yt[0:CS, :])
    halos = [remote(edge.at[d], halo_out.at[d], es.at[d], er.at[d], (r, to)) for d, to in ((0, cup), (1, cdn))]
    class Spread:
        def __init__(self, buf, send, recv):
            def go(first, count, i, to):
                ref = buf.at[pl.ds(first, count)]
                return remote(ref, ref, send.at[i], recv.at[i], to)

            self.far = [go(c, 1, 0, (r, far_c))]
            self.far_in = [go(far_c, 1, 0, (r, far_c))]
            self.y = [go(xy * 2, 2, 1 + d, ypeer[d]) for d in range(3)]
            self.y_in = [go((xx * 4 + lax.rem(yy + 3 - d, 4)) * 2, 2, 1 + d, ypeer[d]) for d in range(3)]
            self.x = [go(xx * 8, 8, 4 + d, xpeer[d]) for d in range(3)]
            self.x_in = [go(lax.rem(xx + 3 - d, 4) * 8, 8, 4 + d, xpeer[d]) for d in range(3)]
            self.sent = self.far + self.y + self.x

    u_spread, g_spread = Spread(ubuf, us, ur), Spread(gbuf, gs, gr)
    ubuf[c] = site_rows(yt)
    begin(u_spread.far)
    begin(halos)

    arrive(pieces_in)
    pieces_twin.start()
    pieces_twin_in.wait_recv()
    for side in (0, 1):
        halves = []
        for h in (0, 1):
            half = pbuf[0, side * 8 + 4 * h]
            for j in range(1, 8):
                half = half + pltpu.roll(pbuf[j % 2, side * 8 + 4 * h + j // 2], 16 * j, 1)
            halves.append(half)
        gbuf[xy * 2 + side] = jnp.concatenate(halves, axis=1)
    begin(g_spread.y)
    rown_t[...] = rown[...].T[0:WIDTH, :]

    def rows_of_t(i):
        part = slice(i * CS, (i + 1) * CS)
        tt[part, :] = nn(rown_t[part, :], yt[...])

    arrive(g_spread.y_in)
    begin(g_spread.x)
    far[2].wait_recv()
    rows_of_t(0)
    tt[0:HALF, :] = tt[0:HALF, :] + tn(rq_in[...], edge[1])
    arrive(u_spread.far_in)
    begin(u_spread.y)
    rows_of_t(1)
    rows_of_t(2)
    outgoing.append(pltpu.make_async_copy(tt, t_out, outs.at[0]))
    outgoing[-1].start()

    arrive(g_spread.x_in)
    gp[...] = gbuf[...].reshape(K, K).T
    outgoing.append(pltpu.make_async_copy(gp, gp_out, outs.at[1]))
    outgoing[-1].start()
    eye = iota((K, K), 0) == iota((K, K), 1)
    shifts = jnp.exp(-2.0 * coupling * field[...].astype(f32)) - 1.0
    pair = gp[...]
    diagonal = jnp.sum(jnp.where(eye, pair, 0.0), axis=0, keepdims=True)
    ratio = shifts / (1.0 + (1.0 - diagonal) * shifts)
    ratio_col = jnp.sum(jnp.where(eye, jnp.broadcast_to(ratio, (K, K)), 0.0), axis=1, keepdims=True)
    powers[0] = jnp.where(eye, 0.0, pair * ratio)
    for step in range(3):
        powers[step + 1] = nn(powers[step], powers[step])
    arrive(u_spread.y_in)
    begin(u_spread.x)
    arrive(rows_in)
    rows_twin.start()
    total = jnp.sum(jnp.sum(powers[3] * powers[3], axis=1, keepdims=True), axis=0, keepdims=True)
    norm[...] = jnp.broadcast_to(total, norm.shape)
    outgoing.append(pltpu.make_async_copy(norm, norm_out, outs.at[2]))
    outgoing[-1].start()

    rows_twin_in.wait_recv()
    for k in range(ROWS):
        vall[k * KR : (k + 1) * KR, :] = vbuf[k % 2, k // 2]
    met = nn(pltpu.roll(vall[:, 384:WIDE], 80, 1)[:, 0:HALF], rq_in[...])
    vall[:, 0:HALF] = vall[:, 0:HALF] + met
    outgoing.append(pltpu.make_async_copy(vall, v_out, outs.at[3]))
    outgoing[-1].start()
    z = vall[:, 0:WIDTH]
    for step in range(4):
        z = z + nn(powers[step], z)
    ws[...] = jnp.zeros_like(ws)
    ws[:, 0:WIDTH] = ratio_col * z
    wt = ws[...].T
    arrive(u_spread.x_in)
    outgoing.append(pltpu.make_async_copy(ubuf, u_out, outs.at[4]))
    outgoing[-1].start()
    for i in range(3):
        part = slice(i * CS, (i + 1) * CS)
        acc[part, :] = tt[part, :] - nn(wt[part, :], ubuf[...].reshape(K, HEIGHT))
        outgoing.append(pltpu.make_async_copy(acc.at[part], acc_out.at[part], outs.at[5 + i]))
        outgoing[-1].start()

    for copy in outgoing:
        copy.wait()
    for copy in near + far + pieces + [pieces_twin] + rows_out + [rows_twin] + u_spread.sent + g_spread.y + g_spread.x:
        copy.wait_send()
    for copy in halos:
        copy.wait()


def finish_kernel(norm_hbm, acc_hbm, halo_hbm, mix_hbm, field_hbm, t_hbm, u_hbm, v_hbm, gp_hbm, out_hbm, norm, acc, halo, mix, field, t, u, v, gp, sem, out_sem):
    first, inner, final = pl.ds(0, HALF), pl.ds(HALF, WIDTH - 2 * HALF), pl.ds(WIDTH - HALF, HALF)
    pairs = [(halo_hbm, halo), (mix_hbm, mix)] + [(acc_hbm.at[part], acc.at[part]) for part in (final, first, inner)]
    pairs.append((norm_hbm, norm))
    loads = [pltpu.make_async_copy(src, dst, sem.at[i]) for i, (src, dst) in enumerate(pairs)]
    stores = [pltpu.make_async_copy(acc.at[part], out_hbm.at[part], out_sem.at[i]) for i, part in enumerate((final, first, inner))]
    for load in loads:
        load.start()
    loads[0].wait()
    loads[1].wait()
    above = tn(mix[...], halo[1])
    loads[2].wait()
    acc[WIDTH - HALF : WIDTH, :] = acc[WIDTH - HALF : WIDTH, :] + above
    stores[0].start()
    loads[3].wait()
    acc[0:HALF, :] = acc[0:HALF, :] + halo[0]
    stores[1].start()
    loads[4].wait()
    stores[2].start()
    loads[5].wait()
    for copy in stores:
        copy.wait()

    @pl.when(jnp.logical_not(norm[0, 0] < series_bound))
    def _():
        for i, (src, dst) in enumerate(((t_hbm, t), (u_hbm, u), (v_hbm, v), (gp_hbm, gp), (field_hbm, field))):
            copy = pltpu.make_async_copy(src, dst, sem.at[i])
            copy.start()
            copy.wait()
        eye = iota((K, K), 0) == iota((K, K), 1)
        ident = jnp.where(eye, 1.0, 0.0)
        shifts = jnp.exp(-2.0 * coupling * field[...].astype(f32)) - 1.0
        gp[...] = ident + (ident - gp[...]) * shifts
        index = iota((K, 1), 0)

        def eliminate(k, carry):
            a = gp[...]
            column = jnp.sum(jnp.where(iota((K, K), 1) == k, a, 0.0), axis=1, keepdims=True)
            size = jnp.where(index >= k, jnp.abs(column), -1.0)
            best = jnp.min(jnp.where(size == jnp.max(size), index, K - 1))
            at_k = jnp.sum(jnp.where(index == k, column, 0.0))
            at_best = jnp.sum(jnp.where(index == best, column, 0.0))
            factors = jnp.where(index == best, at_k, column)
            for ref in (gp, v):
                line = ref[pl.ds(best, 1), :] / at_best
                ref[pl.ds(best, 1), :] = ref[pl.ds(k, 1), :]
                ref[...] = jnp.where(index == k, line, ref[...] - factors * line)
            return carry

        lax.fori_loop(0, K, eliminate, 0)
        shift_col = jnp.sum(jnp.where(eye, jnp.broadcast_to(shifts, (K, K)), 0.0), axis=1, keepdims=True)
        t[...] = t[...] - tn(shift_col * v[:, 0:WIDTH], u[...], highest)
        t[0:HALF, :] = t[0:HALF, :] + halo[0]
        t[WIDTH - HALF : WIDTH, :] = t[WIDTH - HALF : WIDTH, :] + above
        copy = pltpu.make_async_copy(t, out_hbm, sem.at[0])
        copy.start()
        copy.wait()


def on_device(greens, accepted_sites, field_values, left_a, left_b, right_a, right_b):
    hbm = pl.BlockSpec(memory_space=pltpu.HBM)
    shape = lambda *dims: jax.ShapeDtypeStruct(dims, f32)
    v = lambda *dims: pltpu.VMEM(dims, f32)
    dma = lambda *dims: pltpu.SemaphoreType.DMA(dims)
    smem_v = lambda *dims: pltpu.SMEM(dims, jnp.int32)
    field = field_values.reshape(1, K)
    acc, halo, norm, mix, t, u, vv, gp = pl.pallas_call(
        exchange_kernel,
        name="exchange",
        out_shape=[
            shape(WIDTH, HEIGHT), shape(2, HALF, HEIGHT), shape(8, 128), shape(HALF, HALF),
            shape(WIDTH, HEIGHT), shape(COLS, KC, HEIGHT), shape(K, WIDE), shape(K, K),
        ],
        in_specs=[hbm] * 7,
        out_specs=[hbm] * 8,
        scratch_shapes=[
            smem_v(K), pltpu.VMEM((1, K), jnp.int32), v(WIDTH, HEIGHT), v(6, CS, CS), v(6, CS, CS), v(3, CS, CS), v(3, CS, CS),
            v(WIDTH, HEIGHT), v(WIDTH, HEIGHT), v(WIDTH, HEIGHT), v(HEIGHT, TALL), v(HEIGHT, TALL), v(WIDTH, 128),
            v(HALF, WIDTH), v(HALF, WIDTH), v(2, HALF, WIDTH), v(HALF, HALF), v(HALF, HALF), v(HALF, HALF), v(HALF, HALF),
            v(2, WIDTH, 128), v(2, HALF, WIDTH), v(HALF, WIDE), v(WIDTH, WIDE), v(WIDTH, WIDE), v(WIDTH, WIDTH),
            v(2, KR, 128), v(2, KR, 128), v(2, HALF, HEIGHT), v(2, ROWS, KC, 128), v(COLS, KC, HEIGHT), v(2, 8, KR, WIDE), v(K, WIDE),
            v(COLS, KC, K), v(K, K), v(4, K, K), v(K, WIDE), v(8, 128), v(HALF, HALF),
            dma(2), dma(2), dma(6), dma(6), dma(16), dma(17), dma(8), dma(9),
            dma(7), dma(7), dma(7), dma(7), dma(7), dma(9),
        ],
        compiler_params=pltpu.CompilerParams(collective_id=0, has_side_effects=True, vmem_limit_bytes=60 * 2**20),
    )(accepted_sites, field, greens.T, left_a, left_b, right_a, right_b)
    out = pl.pallas_call(
        finish_kernel,
        name="finish",
        out_shape=shape(WIDTH, HEIGHT),
        in_specs=[hbm] * 9,
        out_specs=hbm,
        scratch_shapes=[
            pltpu.SMEM((8, 128), f32), v(WIDTH, HEIGHT), v(2, HALF, HEIGHT), v(HALF, HALF), pltpu.VMEM((1, K), jnp.int32),
            v(WIDTH, HEIGHT), v(K, HEIGHT), v(K, WIDE), v(K, K), dma(6), dma(3),
        ],
        compiler_params=pltpu.CompilerParams(vmem_limit_bytes=60 * 2**20),
    )(norm, acc, halo, mix, field, t, u.reshape(K, HEIGHT), vv, gp)
    return out.T


def solution(mesh):
    return jax.shard_map(
        on_device,
        mesh=mesh,
        in_specs=(
            P("row", "col"),
            P(),
            P(),
            P("row", None, None),
            P("row", None, None),
            P("col", None, None),
            P("col", None, None),
        ),
        out_specs=P("row", "col"),
        check_vma=False,
    )
```

```python
import jax
import jax.numpy as jnp
from jax import lax
from jax.experimental import pallas as pl
from jax.experimental.pallas import tpu as pltpu
from jax.sharding import PartitionSpec as P

MESH = pl.DeviceIdType.MESH
f32 = jnp.float32
high = lax.Precision.HIGH
highest = lax.Precision.HIGHEST
coupling = 0.45
series_bound = 1e-7

CS = 144
HALF = 72
ROWS, COLS = 16, 32
HEIGHT, WIDTH = 864, 432
K = 256
KR, KC = 16, 8
WIDE = 512
TALL = 896
BANDS = ((0, 256, 0, 512), (256, 512, 128, 768), (512, 768, 384, HEIGHT), (768, HEIGHT, 512, HEIGHT))


def dot(a, b, da, db, precision):
    return lax.dot_general(a, b, (((da,), (db,)), ((), ())), precision=precision, preferred_element_type=f32)


def nn(a, b, precision=high):
    return dot(a, b, 1, 0, precision)


def nt(a, b, precision=high):
    return dot(a, b, 1, 1, precision)


def tn(a, b, precision=high):
    return dot(a, b, 0, 0, precision)


def iota(shape, dim):
    return lax.broadcasted_iota(jnp.int32, shape, dim)


def exchange_kernel(
    sites_hbm, field_hbm, gt_hbm, la_hbm, lb_hbm, ra_hbm, rb_hbm,
    acc_out, halo_out, norm_out, mix_out, t_out, u_out, v_out, gp_out,
    sites, field, gt, la, lb, ra, rb, yt, tt, acc, ma, lf, rt, qtop, pbot, top_in, rq_s, rq_in, redge, redge_t, wd, bloc, rown, rown_t,
    xs, x_in, edge, pbuf, ubuf, vbuf, vall, gbuf, gp, powers, ws, norm, mix,
    es, er, ns, nr, ps, pr, vs, vr, us, ur, gs, gr, ins, outs,
):
    r = lax.axis_index("row")
    c = lax.axis_index("col")
    zl, core = r // 2, lax.rem(r, 2)
    zh, xy = lax.rem(c, 2), c // 2
    yy, xx = lax.rem(xy, 4), xy // 4
    rup, rdn = lax.rem(r + 1, ROWS), lax.rem(r + ROWS - 1, ROWS)
    cup, cdn = lax.rem(c + 1, COLS), lax.rem(c + COLS - 1, COLS)
    twin = (r + 1 - 2 * core, c)
    far_c = c + 1 - 2 * zh
    on_line = lambda z: (z * 2 + core, c)
    ypeer = [(r, (xx * 4 + lax.rem(yy + d, 4)) * 2 + zh) for d in (1, 2, 3)]
    xpeer = [(r, (lax.rem(xx + d, 4) * 4 + yy) * 2 + zh) for d in (1, 2, 3)]
    zf = zh * 8 + zl
    ring = [lax.rem(zf + d, 16) for d in range(1, 16)]
    on_ring = lambda z: (lax.rem(z, 8) * 2 + core, xy * 2 + z // 8)
    peers = [(rup, c), (rdn, c), (r, cup), (r, cdn)] + [on_ring(z) for z in ring] + ypeer + xpeer
    barrier = pltpu.get_barrier_semaphore()
    for peer in peers:
        pl.semaphore_signal(barrier, inc=1, device_id=peer, device_id_type=MESH)
    pairs = ((sites_hbm, sites), (gt_hbm, gt), (ra_hbm, ra), (rb_hbm, rb), (la_hbm, la), (lb_hbm, lb), (field_hbm, field))
    loads = [pltpu.make_async_copy(src, dst, ins.at[i]) for i, (src, dst) in enumerate(pairs)]
    for load in loads:
        load.start()
    redge[...] = jnp.zeros_like(redge)
    ma[...] = jnp.zeros_like(ma)
    lf[...] = jnp.zeros_like(lf)
    loads[0].wait()

    def remote(src, dst, send, recv, to):
        return pltpu.make_async_remote_copy(src, dst, send, recv, device_id=to, device_id_type=MESH)

    def begin(copies):
        for copy in copies:
            copy.start()

    def arrive(copies):
        for copy in copies:
            copy.wait_recv()

    lane = iota((1, 128), 1)
    row_site = jnp.full((1, 128), -1, jnp.int32)
    for j in range(KR):
        row_site = jnp.where(lane == j, sites[r * KR + j] - r * HEIGHT, row_site)
    loads[1].wait()
    rt[...] = nn(gt[...], jnp.where(iota((HEIGHT, 128), 0) == row_site, 1.0, 0.0))
    sub = iota((KR, WIDTH), 0)
    where_site = jnp.full((KR, WIDTH), -1, jnp.int32)
    for j in range(KR):
        where_site = jnp.where(sub == j, sites[r * KR + j] - c * WIDTH, where_site)
    x = jnp.where(iota((KR, WIDTH), 1) == where_site, 1.0, 0.0) - rt[...].T[0:KR, :]
    col_site = [jnp.clip(sites[c * KC + j] - c * WIDTH, 0, WIDTH - 1) for j in range(KC)]

    def site_rows(ref):
        shape = (KC, ref.shape[1])
        out = jnp.zeros(shape, f32)
        for j in range(KC):
            out = jnp.where(iota(shape, 0) == j, ref[pl.ds(col_site[j], 1), :], out)
        return out

    pbuf[core, zf] = site_rows(rt)

    loads[2].wait()
    loads[3].wait()
    lower = jnp.concatenate([jnp.zeros((HALF, CS), f32), rb[2, 0:HALF, :]], axis=0)
    redge[0, 2 * CS : 3 * CS, 0:HALF] = nn(ra[2], lower, highest)[:, HALF:CS]
    redge[1, 0:CS, 0:HALF] = ra[0, :, 0:HALF]
    for d in (0, 1):
        redge_t[d] = redge[d].T[0:HALF, :]
        xs[d] = nn(x, redge[d])
    rq_s[...] = rb[2][HALF:CS, HALF:CS]

    pl.semaphore_wait(barrier, len(peers))

    far = [
        remote(xs.at[0], x_in.at[0], ns.at[4], nr.at[4], (r, cup)),
        remote(xs.at[1], x_in.at[1], ns.at[5], nr.at[5], (r, cdn)),
        remote(rq_s, rq_in, ns.at[3], nr.at[3], (r, cup)),
    ]
    begin(far)
    pieces = [remote(pbuf.at[core, zf], pbuf.at[core, zf], ps.at[d], pr.at[zf], on_ring(ring[d])) for d in range(15)]
    pieces_in = [remote(pbuf.at[core, z], pbuf.at[core, z], ps.at[0], pr.at[z], twin) for z in ring]
    pieces_twin = remote(pbuf.at[core], pbuf.at[core], ps.at[15], pr.at[16], twin)
    pieces_twin_in = remote(pbuf.at[1 - core], pbuf.at[1 - core], ps.at[15], pr.at[16], twin)
    begin(pieces)

    mix[...] = rb[2][HALF:CS, 0:HALF]
    outgoing = [pltpu.make_async_copy(mix, mix_out, outs.at[8])]
    outgoing[-1].start()
    loads[4].wait()
    loads[5].wait()
    loads[6].wait()
    pbot[...] = jnp.zeros_like(pbot)
    qtop[...] = jnp.zeros_like(qtop)
    pbot[:, WIDTH : WIDTH + HALF] = lb[5][HALF:CS, HALF:CS]

    for i in range(6):
        ma[i * CS : (i + 1) * CS, i * CS : (i + 1) * CS] = la[i]
    qtop[:, 0:WIDTH] = nt(la[0, 0:HALF, :], gt[:, 0:CS])
    last = nn(lb[5][HALF:CS, 0:HALF], ma[HEIGHT - HALF : HEIGHT, 640:TALL], highest)
    pbot[:, 0:WIDTH] = nt(last[:, 0 : HEIGHT - 640], gt[:, 640:HEIGHT])

    near = [
        remote(pbot, top_in.at[0], ns.at[0], nr.at[0], (rup, c)),
        remote(qtop, top_in.at[1], ns.at[1], nr.at[1], (rdn, c)),
    ]
    begin(near)

    others = [lax.rem(zl + d, 8) for d in range(1, 8)]
    rows_out = [remote(vbuf.at[core, zl], vbuf.at[core, zl], vs.at[d], vr.at[zl], on_line(others[d])) for d in range(7)]
    rows_in = [remote(vbuf.at[core, z], vbuf.at[core, z], vs.at[0], vr.at[z], twin) for z in others]
    rows_twin = remote(vbuf.at[core], vbuf.at[core], vs.at[7], vr.at[8], twin)
    rows_twin_in = remote(vbuf.at[1 - core], vbuf.at[1 - core], vs.at[7], vr.at[8], twin)

    for k in range(5):
        lo, hi = k * CS // 128 * 128, -(-(k + 2) * CS // 128) * 128
        band = slice(HALF + k * CS, HALF + (k + 1) * CS)
        lf[band, lo:hi] = nn(lb[k], ma[band, lo:hi], highest)
    lf[HEIGHT - HALF : HEIGHT, 640:TALL] = nn(lb[5][0:HALF, 0:HALF], ma[HEIGHT - HALF : HEIGHT, 640:TALL], highest)
    bloc[...] = jnp.zeros_like(bloc)
    bloc[HALF : HALF + CS, HALF : HALF + CS] = rb[0]
    bloc[HALF + CS : HALF + 2 * CS, HALF + CS : HALF + 2 * CS] = rb[1]
    bloc[WIDTH - HALF : WIDTH, WIDTH - HALF : WIDTH] = rb[2, 0:HALF, 0:HALF]
    wd[...] = jnp.zeros_like(wd)
    wd[:, WIDTH - HALF : WIDTH] = rb[2, HALF:CS, 0:HALF]
    for i in range(3):
        rown[i * CS : (i + 1) * CS, :] = nn(ra[i], bloc[i * CS : (i + 1) * CS, :], highest)
    right = nn(x, rown[...])
    for a, b, lo, hi in BANDS:
        yt[:, a:b] = nt(gt[:, lo:hi], lf[a:b, lo:hi])
    arrive(far[0:2])
    right += nn(x_in[1][:, 0:HALF], wd[...])
    vbuf[core, zl] = right + jnp.concatenate([x_in[0], jnp.zeros((KR, 256), f32), pltpu.roll(xs[1], 48, 1)], axis=1)
    begin(rows_out)
    arrive(near)
    one = jnp.where(iota((HALF, HALF), 0) == iota((HALF, HALF), 1), 1.0, 0.0)
    yt[:, 0:HALF] = tn(jnp.concatenate([top_in[0, :, 0:WIDTH], nn(pltpu.roll(top_in[0, :, 384:WIDE], 80, 1)[:, 0:HALF], qtop[:, 0:WIDTH])], axis=0), jnp.concatenate([one, one], axis=0))
    tail = jnp.concatenate([jnp.zeros((24, HALF), f32), lb[5][0:HALF, HALF:CS]], axis=0)
    yt[:, 768:HEIGHT] = yt[:, 768:HEIGHT] + tn(top_in[1, :, 0:WIDTH], tail.T)

    edge[0] = nn(redge_t[0, :, 256:WIDTH], yt[256:WIDTH, :])
    edge[1] = nn(redge_t[1, :, 0:CS], yt[0:CS, :])
    halos = [remote(edge.at[d], halo_out.at[d], es.at[d], er.at[d], (r, to)) for d, to in ((0, cup), (1, cdn))]
    class Spread:
        def __init__(self, buf, send, recv):
            def go(first, count, i, to):
                ref = buf.at[pl.ds(first, count)]
                return remote(ref, ref, send.at[i], recv.at[i], to)

            self.far = [go(c, 1, 0, (r, far_c))]
            self.far_in = [go(far_c, 1, 0, (r, far_c))]
            self.y = [go(xy * 2, 2, 1 + d, ypeer[d]) for d in range(3)]
            self.y_in = [go((xx * 4 + lax.rem(yy + 3 - d, 4)) * 2, 2, 1 + d, ypeer[d]) for d in range(3)]
            self.x = [go(xx * 8, 8, 4 + d, xpeer[d]) for d in range(3)]
            self.x_in = [go(lax.rem(xx + 3 - d, 4) * 8, 8, 4 + d, xpeer[d]) for d in range(3)]
            self.sent = self.far + self.y + self.x

    u_spread, g_spread = Spread(ubuf, us, ur), Spread(gbuf, gs, gr)
    ubuf[c] = site_rows(yt)
    begin(u_spread.far)
    begin(halos)

    arrive(pieces_in)
    pieces_twin.start()
    pieces_twin_in.wait_recv()
    for side in (0, 1):
        halves = []
        for h in (0, 1):
            half = pbuf[0, side * 8 + 4 * h]
            for j in range(1, 8):
                half = half + pltpu.roll(pbuf[j % 2, side * 8 + 4 * h + j // 2], 16 * j, 1)
            halves.append(half)
        gbuf[xy * 2 + side] = jnp.concatenate(halves, axis=1)
    begin(g_spread.y)
    rown_t[...] = rown[...].T[0:WIDTH, :]

    def rows_of_t(i):
        part = slice(i * CS, (i + 1) * CS)
        tt[part, :] = nn(rown_t[part, :], yt[...])

    arrive(g_spread.y_in)
    begin(g_spread.x)
    far[2].wait_recv()
    rows_of_t(0)
    tt[0:HALF, :] = tt[0:HALF, :] + tn(rq_in[...], edge[1])
    arrive(u_spread.far_in)
    begin(u_spread.y)
    rows_of_t(1)
    rows_of_t(2)
    outgoing.append(pltpu.make_async_copy(tt, t_out, outs.at[0]))
    outgoing[-1].start()

    arrive(g_spread.x_in)
    gp[...] = gbuf[...].reshape(K, K).T
    outgoing.append(pltpu.make_async_copy(gp, gp_out, outs.at[1]))
    outgoing[-1].start()
    eye = iota((K, K), 0) == iota((K, K), 1)
    shifts = jnp.exp(-2.0 * coupling * field[...].astype(f32)) - 1.0
    pair = gp[...]
    diagonal = jnp.sum(jnp.where(eye, pair, 0.0), axis=0, keepdims=True)
    ratio = shifts / (1.0 + (1.0 - diagonal) * shifts)
    ratio_col = jnp.sum(jnp.where(eye, jnp.broadcast_to(ratio, (K, K)), 0.0), axis=1, keepdims=True)
    powers[0] = jnp.where(eye, 0.0, pair * ratio)
    for step in range(3):
        powers[step + 1] = nn(powers[step], powers[step])
    arrive(u_spread.y_in)
    begin(u_spread.x)
    arrive(rows_in)
    rows_twin.start()
    total = jnp.sum(jnp.sum(powers[3] * powers[3], axis=1, keepdims=True), axis=0, keepdims=True)
    norm[...] = jnp.broadcast_to(total, norm.shape)
    outgoing.append(pltpu.make_async_copy(norm, norm_out, outs.at[2]))
    outgoing[-1].start()

    rows_twin_in.wait_recv()
    for k in range(ROWS):
        vall[k * KR : (k + 1) * KR, :] = vbuf[k % 2, k // 2]
    met = nn(pltpu.roll(vall[:, 384:WIDE], 80, 1)[:, 0:HALF], rq_in[...])
    vall[:, 0:HALF] = vall[:, 0:HALF] + met
    outgoing.append(pltpu.make_async_copy(vall, v_out, outs.at[3]))
    outgoing[-1].start()
    z = vall[:, 0:WIDTH]
    for step in range(4):
        z = z + nn(powers[step], z)
    ws[...] = jnp.zeros_like(ws)
    ws[:, 0:WIDTH] = ratio_col * z
    wt = ws[...].T
    arrive(u_spread.x_in)
    outgoing.append(pltpu.make_async_copy(ubuf, u_out, outs.at[4]))
    outgoing[-1].start()
    for i in range(3):
        part = slice(i * CS, (i + 1) * CS)
        acc[part, :] = tt[part, :] - nn(wt[part, :], ubuf[...].reshape(K, HEIGHT))
        outgoing.append(pltpu.make_async_copy(acc.at[part], acc_out.at[part], outs.at[5 + i]))
        outgoing[-1].start()

    for copy in outgoing:
        copy.wait()
    for copy in near + far + pieces + [pieces_twin] + rows_out + [rows_twin] + u_spread.sent + g_spread.y + g_spread.x:
        copy.wait_send()
    for copy in halos:
        copy.wait()


def finish_kernel(norm_hbm, acc_hbm, halo_hbm, mix_hbm, field_hbm, t_hbm, u_hbm, v_hbm, gp_hbm, out_hbm, norm, acc, halo, mix, field, t, u, v, gp, sem, out_sem):
    first, inner, final = pl.ds(0, HALF), pl.ds(HALF, WIDTH - 2 * HALF), pl.ds(WIDTH - HALF, HALF)
    pairs = [(halo_hbm, halo), (mix_hbm, mix)] + [(acc_hbm.at[part], acc.at[part]) for part in (final, first, inner)]
    pairs.append((norm_hbm, norm))
    loads = [pltpu.make_async_copy(src, dst, sem.at[i]) for i, (src, dst) in enumerate(pairs)]
    stores = [pltpu.make_async_copy(acc.at[part], out_hbm.at[part], out_sem.at[i]) for i, part in enumerate((final, first, inner))]
    for load in loads:
        load.start()
    loads[0].wait()
    loads[1].wait()
    above = tn(mix[...], halo[1])
    loads[2].wait()
    acc[WIDTH - HALF : WIDTH, :] = acc[WIDTH - HALF : WIDTH, :] + above
    stores[0].start()
    loads[3].wait()
    acc[0:HALF, :] = acc[0:HALF, :] + halo[0]
    stores[1].start()
    loads[4].wait()
    stores[2].start()
    loads[5].wait()
    for copy in stores:
        copy.wait()

    @pl.when(jnp.logical_not(norm[0, 0] < series_bound))
    def _():
        for i, (src, dst) in enumerate(((t_hbm, t), (u_hbm, u), (v_hbm, v), (gp_hbm, gp), (field_hbm, field))):
            copy = pltpu.make_async_copy(src, dst, sem.at[i])
            copy.start()
            copy.wait()
        eye = iota((K, K), 0) == iota((K, K), 1)
        ident = jnp.where(eye, 1.0, 0.0)
        shifts = jnp.exp(-2.0 * coupling * field[...].astype(f32)) - 1.0
        gp[...] = ident + (ident - gp[...]) * shifts
        index = iota((K, 1), 0)

        def eliminate(k, carry):
            a = gp[...]
            column = jnp.sum(jnp.where(iota((K, K), 1) == k, a, 0.0), axis=1, keepdims=True)
            size = jnp.where(index >= k, jnp.abs(column), -1.0)
            best = jnp.min(jnp.where(size == jnp.max(size), index, K - 1))
            at_k = jnp.sum(jnp.where(index == k, column, 0.0))
            at_best = jnp.sum(jnp.where(index == best, column, 0.0))
            factors = jnp.where(index == best, at_k, column)
            for ref in (gp, v):
                line = ref[pl.ds(best, 1), :] / at_best
                ref[pl.ds(best, 1), :] = ref[pl.ds(k, 1), :]
                ref[...] = jnp.where(index == k, line, ref[...] - factors * line)
            return carry

        lax.fori_loop(0, K, eliminate, 0)
        shift_col = jnp.sum(jnp.where(eye, jnp.broadcast_to(shifts, (K, K)), 0.0), axis=1, keepdims=True)
        t[...] = t[...] - tn(shift_col * v[:, 0:WIDTH], u[...], highest)
        t[0:HALF, :] = t[0:HALF, :] + halo[0]
        t[WIDTH - HALF : WIDTH, :] = t[WIDTH - HALF : WIDTH, :] + above
        copy = pltpu.make_async_copy(t, out_hbm, sem.at[0])
        copy.start()
        copy.wait()


def on_device(greens, accepted_sites, field_values, left_a, left_b, right_a, right_b):
    hbm = pl.BlockSpec(memory_space=pltpu.HBM)
    shape = lambda *dims: jax.ShapeDtypeStruct(dims, f32)
    v = lambda *dims: pltpu.VMEM(dims, f32)
    dma = lambda *dims: pltpu.SemaphoreType.DMA(dims)
    smem_v = lambda *dims: pltpu.SMEM(dims, jnp.int32)
    field = field_values.reshape(1, K)
    acc, halo, norm, mix, t, u, vv, gp = pl.pallas_call(
        exchange_kernel,
        name="exchange",
        out_shape=[
            shape(WIDTH, HEIGHT), shape(2, HALF, HEIGHT), shape(8, 128), shape(HALF, HALF),
            shape(WIDTH, HEIGHT), shape(COLS, KC, HEIGHT), shape(K, WIDE), shape(K, K),
        ],
        in_specs=[hbm] * 7,
        out_specs=[hbm] * 8,
        scratch_shapes=[
            smem_v(K), pltpu.VMEM((1, K), jnp.int32), v(WIDTH, HEIGHT), v(6, CS, CS), v(6, CS, CS), v(3, CS, CS), v(3, CS, CS),
            v(WIDTH, HEIGHT), v(WIDTH, HEIGHT), v(WIDTH, HEIGHT), v(HEIGHT, TALL), v(HEIGHT, TALL), v(WIDTH, 128),
            v(HALF, WIDE), v(HALF, WIDE), v(2, HALF, WIDE), v(HALF, HALF), v(HALF, HALF),
            v(2, WIDTH, 128), v(2, HALF, WIDTH), v(HALF, WIDE), v(WIDTH, WIDE), v(WIDTH, WIDE), v(WIDTH, WIDTH),
            v(2, KR, 128), v(2, KR, 128), v(2, HALF, HEIGHT), v(2, ROWS, KC, 128), v(COLS, KC, HEIGHT), v(2, 8, KR, WIDE), v(K, WIDE),
            v(COLS, KC, K), v(K, K), v(4, K, K), v(K, WIDE), v(8, 128), v(HALF, HALF),
            dma(2), dma(2), dma(6), dma(6), dma(16), dma(17), dma(8), dma(9),
            dma(7), dma(7), dma(7), dma(7), dma(7), dma(9),
        ],
        compiler_params=pltpu.CompilerParams(collective_id=0, has_side_effects=True, vmem_limit_bytes=60 * 2**20),
    )(accepted_sites, field, greens.T, left_a, left_b, right_a, right_b)
    out = pl.pallas_call(
        finish_kernel,
        name="finish",
        out_shape=shape(WIDTH, HEIGHT),
        in_specs=[hbm] * 9,
        out_specs=hbm,
        scratch_shapes=[
            pltpu.SMEM((8, 128), f32), v(WIDTH, HEIGHT), v(2, HALF, HEIGHT), v(HALF, HALF), pltpu.VMEM((1, K), jnp.int32),
            v(WIDTH, HEIGHT), v(K, HEIGHT), v(K, WIDE), v(K, K), dma(6), dma(3),
        ],
        compiler_params=pltpu.CompilerParams(vmem_limit_bytes=60 * 2**20),
    )(norm, acc, halo, mix, field, t, u.reshape(K, HEIGHT), vv, gp)
    return out.T


def solution(mesh):
    return jax.shard_map(
        on_device,
        mesh=mesh,
        in_specs=(
            P("row", "col"),
            P(),
            P(),
            P("row", None, None),
            P("row", None, None),
            P("col", None, None),
            P("col", None, None),
        ),
        out_specs=P("row", "col"),
        check_vma=False,
    )
```
